32 devices in a mesh: seq: 4 (over y, x), chan: 8 (over z, core).
Axes of the slice: x: 2, y: 2, z: 4, core: 2. Of those that a mesh axis runs over, the one named last changes fastest.
Arguments:
- hidden: bfloat16 [2, 8192, 2048], P(None, ('seq', 'chan')), may hold values from -6 to 6
- out_grad: bfloat16 [2, 8192, 2048], P(None, ('seq', 'chan')), may hold values from -6 to 6
- modality: int32 [2, 8192], P(None, 'seq'), may hold values from 0 to 2, as said below
- lengths: int32 [2, 4, 5], P(None, 'seq'), may hold values from 1 to 1024, as said below
- in_weight: bfloat16 [3, 2048, 2, 4096], P(None, 'seq', None, 'chan'), may hold values from -0.125 to 0.125
- x_weight: bfloat16 [3, 4096, 160], P(None, 'chan', 'seq'), may hold values from -0.09375 to 0.09375
- dt_weight: bfloat16 [3, 128, 4096], P(None, 'seq', 'chan'), may hold values from -0.5 to 0.5
- out_weight: bfloat16 [3, 4096, 2048], P(None, 'chan', 'seq'), may hold values from -0.375 to 0.375
- conv_weight: float32 [4, 4096], P(None, 'chan'), may hold values from -3 to 3
- conv_bias: float32 [4096], P('chan'), may hold values from -4 to 4
- a_log: float32 [16, 4096], P(None, 'chan'), may hold values from 0 to 2.7
- d_skip: float32 [4096], P('chan'), may hold values from 0.5 to 1.5
- dt_bias: float32 [4096], P('chan'), may hold values from -4.5 to -2
- norm_gain: float32 [2048], P('chan'), may hold values from 0.5 to 1.5
Outputs:
- out: bfloat16 [2, 8192, 2048], P(None, ('seq', 'chan'))
- hidden_grad: float32 [2, 8192, 2048], P(None, ('seq', 'chan'))
- in_weight_grad: float32 [3, 2048, 2, 4096], P(None, 'seq', None, 'chan')
- x_weight_grad: float32 [3, 4096, 160], P(None, 'chan', 'seq')
- dt_weight_grad: float32 [3, 128, 4096], P(None, 'seq', 'chan')
- out_weight_grad: float32 [3, 4096, 2048], P(None, 'chan', 'seq')
- conv_weight_grad: float32 [4, 4096], P(None, 'chan')
- conv_bias_grad: float32 [4096], P('chan')
- a_log_grad: float32 [16, 4096], P(None, 'chan')
- d_skip_grad: float32 [4096], P('chan')
- dt_bias_grad: float32 [4096], P('chan')
- norm_gain_grad: float32 [2048], P('chan')
The draws below stay inside these ranges and needn't reach their ends.
Inputs may be any that keep to these rules, and one draw needn't show every extreme that they name: Each group's entries are 4 sequence lengths in token order and then the padding at the group's end; they sum to 2048; the longest sequence has exactly 1024 tokens and the padding at most 128. `modality`: constant over aligned runs of 1024 tokens.
All inputs are finite; a program needn't handle non-finite values.
Results may differ from the reference program's by a relative error of at most 0.011.
Values may be sent and summed in bfloat16 or wider, within the bound.
A program may use at most 1 GiB of HBM per device.

```python
import jax
import jax.numpy as jnp
from jax import lax

D = 2048
E = 4096
N = 16
K = 4
R = 128
MODES = 3
MICRO = 2
SEQS = 4
MBLK = 1024
GROUP = 2048
LONGEST = 1024
PADMAX = 128
SEQ_GROUPS = 4
TOKENS = 8192
XCOLS = 160


def draw_lengths(key, part):
    keys = jax.random.split(key, MICRO * SEQ_GROUPS)

    def single(one):
        first, second, third = jax.random.split(one, 3)
        padding = jax.random.randint(first, (), 1, PADMAX + 1)
        spread = GROUP - LONGEST - padding - (SEQS - 1)
        raw = jax.random.randint(second, (SEQS - 1,), 1, 32)
        weights = raw * raw
        total = jnp.sum(weights)
        marks = jnp.concatenate([jnp.zeros((1,), jnp.int32), spread * jnp.cumsum(weights) // total])
        pieces = 1 + marks[1:] - marks[:-1]
        place = jax.random.randint(third, (), 0, SEQS)
        slots = jnp.arange(SEQS)
        after = jnp.concatenate([pieces, jnp.zeros((1,), jnp.int32)])
        before = jnp.concatenate([jnp.zeros((1,), jnp.int32), pieces])
        seqlens = jnp.where(slots < place, after, jnp.where(slots == place, LONGEST, before))
        return jnp.concatenate([seqlens, padding[None]]).astype(jnp.int32)
    return jax.vmap(single)(keys).reshape(MICRO, SEQ_GROUPS, SEQS + 1)


def draw_modality(key, part):
    runs = jax.random.randint(key, (MICRO, TOKENS // MBLK), 0, MODES)
    return jnp.repeat(runs, MBLK, axis=1).astype(jnp.int32)


def steps_of(stream_key, dims, shards, smallest, largest):
    level, own = 1.0, jax.random.fold_in(stream_key, 6)
    for axis_at, shards_of in shards:
        heights = jnp.exp(jax.random.uniform(jax.random.fold_in(own, axis_at), (shards_of,), jnp.float32, smallest / len(shards), largest / len(shards)))
        level = level * jnp.repeat(heights, dims[axis_at] // shards_of).reshape([-1 if axis == axis_at else 1 for axis in range(len(dims))])
    return level


def scatter_about(rng, dims, deviation, reach, shards=(), dtype=jnp.bfloat16):
    level = steps_of(rng, dims, shards, -0.22, 0.18) if shards else 1.0
    drawn = jax.random.normal(rng, dims, jnp.float32) * deviation * level
    return jnp.minimum(jnp.maximum(drawn, -reach), reach).astype(dtype)


def setup_inputs(seed: int = 0) -> dict:
    key_of = jax.random.split(jax.random.key(seed), 15)
    return {
        "hidden": scatter_about(key_of[0], (MICRO, TOKENS, D), 1.0, 6.0, ((1, 32),)),
        "out_grad": scatter_about(key_of[1], (MICRO, TOKENS, D), 1.0, 6.0, ((1, 32),)),
        "modality": draw_modality(jax.random.fold_in(key_of[14], 71), 0),
        "lengths": draw_lengths(jax.random.fold_in(key_of[14], 71), 0),
        "in_weight": scatter_about(key_of[4], (MODES, D, 2, E), D ** -0.5, 0.125, ((1, 4), (3, 8))),
        "x_weight": scatter_about(key_of[5], (MODES, E, XCOLS), E ** -0.5, 0.09375, ((1, 8), (2, 4))),
        "dt_weight": scatter_about(key_of[6], (MODES, R, E), R ** -0.5, 0.5, ((1, 4), (2, 8))),
        "out_weight": scatter_about(key_of[7], (MODES, E, D), (E // 16) ** -0.5, 0.375, ((1, 8), (2, 4))),
        "conv_weight": scatter_about(key_of[8], (K, E), K ** -0.5, 3.0, ((1, 8),), jnp.float32),
        "conv_bias": scatter_about(key_of[9], (E,), 0.3, 4.0, ((0, 8),), jnp.float32),
        "a_log": jnp.clip(2.7 * jax.random.uniform(key_of[10], (N, E), jnp.float32) ** steps_of(key_of[10], (N, E), ((1, 8),), -0.2, 0.2), 0.0, 2.7),
        "d_skip": jnp.clip(0.5 + 1.0 * jax.random.uniform(key_of[11], (E,), jnp.float32) ** steps_of(key_of[11], (E,), ((0, 8),), -0.2, 0.2), 0.5, 1.5),
        "dt_bias": jnp.clip(-4.5 + 2.5 * jax.random.uniform(key_of[12], (E,), jnp.float32) ** steps_of(key_of[12], (E,), ((0, 8),), -0.2, 0.2), -4.5, -2.0),
        "norm_gain": jnp.clip(1.0 + 0.1 * jax.random.normal(key_of[13], (D,), jnp.float32), 0.5, 1.5),
    }


@jax.custom_vjp
def low(v):
    return lax.optimization_barrier(v.astype(jnp.bfloat16)).astype(jnp.float32)

@jax.custom_vjp
def low_back(v):
    return v

def low_keep(v):
    return (low(v), None)

def low_pass(kept, grad):
    return (grad,)

def back_keep(v):
    return (v, None)

def back_low(kept, grad):
    return (low(grad),)
low.defvjp(low_keep, low_pass)
low_back.defvjp(back_keep, back_low)
highest = lax.Precision.HIGHEST

def matmul(left, right):
    return jnp.dot(left, right, preferred_element_type=jnp.float32, precision=highest)

def token_layout(lens, count):
    ends = jnp.cumsum(lens)
    places = jnp.arange(count)
    begins = lax.optimization_barrier(jnp.sum(jnp.where(ends[None, :] <= places[:, None], lens[None, :], 0), axis=1))
    position = places - begins
    valid = (places < ends[-2]).astype(jnp.float32)
    return (position, valid)

def selective(delta, b_in, c_out, xval, keep, rate):
    count, inner = delta.shape
    width = min(256, count)

    def block_fn(carry, pieces):

        def one_step(state, item):
            step_dt, step_b, step_c, step_x, step_keep = item
            state = jnp.exp(step_dt[None, :] * rate) * step_keep * state + step_dt[None, :] * step_b[:, None] * step_x[None, :]
            return (state, lax.optimization_barrier(jnp.sum(step_c[:, None] * state, axis=0)))
        return lax.scan(one_step, carry, pieces)
    pieces = tuple((v.reshape((count // width, width) + v.shape[1:]) for v in (delta, b_in, c_out, xval, keep)))
    start = jnp.zeros(rate.shape, jnp.float32)
    final, outputs = lax.scan(jax.checkpoint(block_fn), start, pieces)
    return outputs.reshape(count, inner)

def group_forward(params, hidden, kinds, lens):
    in_w, x_w, dt_w, out_w, conv_w, conv_b, a_log, d_skip, dt_b, gain = params
    count = hidden.shape[0]
    inner = in_w.shape[3]
    rank = dt_w.shape[1]
    nstate = a_log.shape[0]
    scale = lax.rsqrt(lax.optimization_barrier(jnp.mean(hidden * hidden, axis=1, keepdims=True)) + 1e-05)
    normed = low(hidden * scale * gain[None, :])
    onehot = (kinds[:, None] == jnp.arange(MODES)[None, :]).astype(jnp.float32)
    mixed = sum((onehot[:, m:m + 1] * matmul(normed, in_w[m].reshape(-1, 2 * inner)) for m in range(MODES)))
    x_in = low_back(mixed[:, :inner])
    gate_in = low_back(mixed[:, inner:])
    position, valid = token_layout(lens, count)
    conv = jnp.zeros_like(x_in) + conv_b[None, :]
    for lag in range(conv_w.shape[0]):
        moved = jnp.concatenate([jnp.zeros((lag, inner), jnp.float32), x_in[:count - lag]], axis=0)
        conv = conv + conv_w[lag][None, :] * moved * (position >= lag).astype(jnp.float32)[:, None]
    xc = low(jax.nn.silu(conv))
    proj = low_back(sum((onehot[:, m:m + 1] * matmul(xc, x_w[m]) for m in range(MODES))))
    dt_low = low(proj[:, :rank])
    b_in = proj[:, rank:rank + nstate]
    c_out = proj[:, rank + nstate:]
    dt_pre = low_back(sum((onehot[:, m:m + 1] * matmul(dt_low, dt_w[m]) for m in range(MODES))) + dt_b[None, :])
    delta = jax.nn.softplus(dt_pre)
    rate = -jnp.exp(a_log)
    keep = (position > 0).astype(jnp.float32)
    scanned = selective(delta, b_in, c_out, xc, keep, rate) + d_skip[None, :] * xc
    y_out = low(scanned * jax.nn.silu(gate_in) * valid[:, None])
    return hidden + sum((onehot[:, m:m + 1] * matmul(y_out, out_w[m]) for m in range(MODES)))

def reference(hidden, out_grad, modality, lengths, in_weight, x_weight, dt_weight, out_weight, conv_weight, conv_bias, a_log, d_skip, dt_bias, norm_gain):
    micro, tokens, width = hidden.shape
    groups = lengths.shape[1]
    floats = tuple((v.astype(jnp.float32) for v in (hidden, in_weight, x_weight, dt_weight, out_weight, conv_weight, conv_bias, a_log, d_skip, dt_bias, norm_gain)))
    kinds_all = modality.reshape(micro * groups, tokens // groups)
    lens_all = lengths.reshape(micro * groups, lengths.shape[2])

    def forward(*values):
        hid = values[0]
        params = values[1:]
        hid_groups = hid.reshape(micro * groups, tokens // groups, width)

        def one_group(item):
            return group_forward(params, item[0], item[1], item[2])
        outputs = lax.map(jax.checkpoint(one_group), (hid_groups, kinds_all, lens_all))
        return outputs.reshape(micro, tokens, width)
    result, pull = jax.vjp(forward, *floats)
    grads = pull(out_grad.astype(jnp.float32))
    return (result.astype(jnp.bfloat16), grads[0], grads[1], grads[2], grads[3], grads[4], grads[5], grads[6], grads[7], grads[8], grads[9], grads[10])
```

```python
import functools

import jax
import jax.numpy as jnp
from jax import lax
from jax.experimental import pallas as pl
from jax.experimental.pallas import tpu as pltpu
from jax.sharding import PartitionSpec as P

MODES = 3
MBLK = 1024
LOG2E = 1.4426950408889634
RESET = 1.0e4
CHUNKS = 8
UNROLL = 4

f32, bf16 = jnp.float32, jnp.bfloat16
HBM = pl.BlockSpec(memory_space=pl.ANY)
VMEM = pl.BlockSpec(memory_space=pltpu.VMEM)


def sds(shape, dtype):
    return jax.ShapeDtypeStruct(shape, dtype)


def cost(flops, nbytes, trans=0):
    return pl.CostEstimate(flops=int(flops), bytes_accessed=int(nbytes), transcendentals=int(trans))


def dsilu(value):
    sig = jax.nn.sigmoid(value)
    return sig * (1.0 + value * (1.0 - sig))


def gmm_kernel(trans, kinds, x, w, out):
    dims = (((1,), (1,)), ((), ())) if trans else (((1,), (0,)), ((), ()))
    out[...] = lax.dot_general(x[...], w[0], dims, preferred_element_type=f32).astype(out.dtype)


def gmm(kinds, x, w, trans, dtype, name, rb=512, cb=512):
    T, K = x.shape
    C = w.shape[1] if trans else w.shape[2]
    cb = min(cb, C)
    per = MBLK // rb
    wspec = (
        pl.BlockSpec((1, cb, K), lambda t, c, r, kinds: (kinds[t], c, 0))
        if trans
        else pl.BlockSpec((1, K, cb), lambda t, c, r, kinds: (kinds[t], 0, c))
    )
    return pl.pallas_call(
        functools.partial(gmm_kernel, trans),
        grid_spec=pltpu.PrefetchScalarGridSpec(
            num_scalar_prefetch=1,
            grid=(T // MBLK, C // cb, per),
            in_specs=[pl.BlockSpec((rb, K), lambda t, c, r, kinds: (t * per + r, 0)), wspec],
            out_specs=pl.BlockSpec((rb, cb), lambda t, c, r, kinds: (t * per + r, c)),
        ),
        out_shape=sds((T, C), dtype),
        compiler_params=pltpu.CompilerParams(vmem_limit_bytes=40 << 20),
        cost_estimate=cost(2 * T * K * C, 2 * T * K + 4 * K * C + 4 * T * C),
        name=name,
    )(kinds, x, w)


def wgrad_kernel(nm, plan, *refs):
    acc = refs[-1]
    out = refs[-2]
    step = pl.program_id(1)

    @pl.when(plan[2, step] == 0)
    def _():
        acc[...] = jnp.zeros_like(acc)

    for i in range(nm):

        @pl.when(plan[2, step] == i + 1)
        def _():
            acc[...] += lax.dot_general(
                refs[2 * i][...], refs[2 * i + 1][...], (((0,), (0,)), ((), ())), preferred_element_type=f32
            )

    out[0] = acc[...].astype(out.dtype)


def wgrad_plan(kinds):
    nm, nt = kinds.shape
    flat = kinds.reshape(-1)
    n = nm * nt
    ids = jnp.arange(n)
    modes = jnp.arange(MODES)
    first = jnp.min(jnp.where(flat[None, :] == modes[:, None], ids[None, :], n), axis=1)
    first = jnp.where(first == n, 0, first)
    key = jnp.concatenate([modes * (n + 1), flat * (n + 1) + 1 + ids])
    mode = jnp.concatenate([modes, flat])
    tile = jnp.concatenate([first, ids])
    live = jnp.concatenate([jnp.zeros((MODES,), jnp.int32), ids // nt + 1])
    rank = jnp.sum((key[None, :] < key[:, None]).astype(jnp.int32), axis=1)
    place = (rank[None, :] == jnp.arange(MODES + n)[:, None]).astype(jnp.int32)

    def order(v):
        return jnp.sum(place * v[None, :], axis=1)

    rows = [order(mode), order(tile), order(live)]
    for i in range(nm):
        rows.append(jnp.clip(order(tile) - i * nt, 0, nt - 1))
    return jnp.stack(rows).astype(jnp.int32)


def wgrad(plan, lefts, rights, name, db):
    nm = len(lefts)
    D, C = lefts[0].shape[1], rights[0].shape[1]
    specs, args = [], []
    for i in range(nm):
        specs.append(pl.BlockSpec((MBLK, db), lambda d, s, plan, i=i: (plan[3 + i, s], d)))
        specs.append(pl.BlockSpec((MBLK, C), lambda d, s, plan, i=i: (plan[3 + i, s], 0)))
        args += [lefts[i], rights[i]]
    T = nm * lefts[0].shape[0]
    return pl.pallas_call(
        functools.partial(wgrad_kernel, nm),
        grid_spec=pltpu.PrefetchScalarGridSpec(
            num_scalar_prefetch=1,
            grid=(D // db, plan.shape[1]),
            in_specs=specs,
            out_specs=pl.BlockSpec((1, db, C), lambda d, s, plan: (plan[0, s], d, 0)),
            scratch_shapes=[pltpu.VMEM((db, C), f32)],
        ),
        out_shape=sds((MODES, D, C), bf16),
        compiler_params=pltpu.CompilerParams(vmem_limit_bytes=48 << 20),
        cost_estimate=cost(2 * T * D * C, 2 * T * (D + C * (D // db)) + 2 * MODES * D * C),
        name=name,
    )(plan, *args)


def chain(ends, total, back):
    row = lax.broadcasted_iota(jnp.int32, ends.shape, 0)
    for k in (1, 2, 4):
        shift = CHUNKS - k if back else k
        ok = (row < CHUNKS - k) if back else (row >= k)
        ends = ends + total * jnp.where(ok, pltpu.roll(ends, shift, 0), 0.0)
        total = total * jnp.where(ok, pltpu.roll(total, shift, 0), 1.0)
    shift = CHUNKS - 1 if back else 1
    ok = (row < CHUNKS - 1) if back else (row >= 1)
    return jnp.where(ok, pltpu.roll(ends, shift, 0), 0.0)


def scan_kernel(
    S, NG, ddec_h, dx_h, ds_h, bc, rate2, rate, y_h, gb_h, fr_h, db, dc, drate,
    ddec, dx, ds, y, gb, fr, p_scr, bb, cb, q, sems
):
    NN, L = rate.shape
    KT = L // 128
    copies = []
    for a, (src, dst) in enumerate(((ddec_h, ddec), (dx_h, dx), (ds_h, ds))):
        for c in range(CHUNKS):
            copies.append(
                pltpu.make_async_copy(src.at[pl.ds(c * S, S), :], dst.at[:, c, :], sems.at[a, c])
            )
    for cp in copies:
        cp.start()
    db[...] = jnp.zeros_like(db)
    dc[...] = jnp.zeros_like(dc)
    y[...] = jnp.zeros_like(y)
    gb[...] = jnp.zeros_like(gb)
    fr[...] = jnp.zeros_like(fr)
    for cp in copies:
        cp.wait()

    def rows(s):
        return pl.ds(pl.multiple_of(s * 8, 8), 8)

    def wide(v):
        return jnp.concatenate([v] * KT, axis=1)

    def fold(v):
        return sum(v[:, 128 * i : 128 * i + 128] for i in range(KT))

    def loop(body, init):
        def outer(k, carry):
            for u in range(UNROLL):
                carry = body(k * UNROLL + u, carry)
            return carry

        return lax.fori_loop(0, S // UNROLL, outer, init)

    dsum = lax.fori_loop(0, S, lambda s, a: a + ddec[s], jnp.zeros((8, L), f32))

    def group(g, _):
        kk = lax.broadcasted_iota(jnp.int32, (2 * NN, NG * 128), 0)
        ln = lax.broadcasted_iota(jnp.int32, (2 * NN, NG * 128), 1) // 128
        Xb = jnp.where(kk == g * NG + ln, 1.0, 0.0).astype(bf16)
        Xc = jnp.where(kk == NN + g * NG + ln, 1.0, 0.0).astype(bf16)
        rr = lax.broadcasted_iota(jnp.int32, (NG * 128, 128), 0) // 128
        cc = lax.broadcasted_iota(jnp.int32, (NG * 128, 128), 1)
        R = jnp.where(cc == rr + g * NG, 1.0, 0.0).astype(bf16)

        def expand(i, _):
            at = pl.ds(pl.multiple_of(i * 256, 256), 256)
            v = bc[at, :]
            hi = v.astype(bf16)
            lo = (v - hi.astype(f32)).astype(bf16)
            for X, o in ((Xb, bb), (Xc, cb)):
                o[at, :] = jnp.dot(hi, X, preferred_element_type=f32) + jnp.dot(
                    lo, X, preferred_element_type=f32
                )
            return 0

        lax.fori_loop(0, S * 8 // 256, expand, 0)

        def reduce(out):
            def body(i, _):
                at = pl.ds(pl.multiple_of(i * 256, 256), 256)
                out[at, :] += jnp.dot(q[at, :].astype(bf16), R, preferred_element_type=f32)
                return 0

            lax.fori_loop(0, S * 8 // 256, body, 0)

        r2 = [jnp.broadcast_to(rate2[pl.ds(g * NG + n, 1), :], (8, L)) for n in range(NG)]
        rt = [jnp.broadcast_to(rate[pl.ds(g * NG + n, 1), :], (8, L)) for n in range(NG)]
        total = [jnp.exp2(dsum * r2[n]) for n in range(NG)]
        zero = tuple(jnp.zeros((8, L), f32) for _ in range(NG))
        cols = [slice(128 * n, 128 * n + 128) for n in range(NG)]

        def ahead(s, st):
            d, x, b = ddec[s], dx[s], bb[rows(s), :]
            return tuple(
                jnp.exp2(d * r2[n]) * st[n] + x * wide(b[:, cols[n]]) for n in range(NG)
            )

        st = loop(ahead, zero)
        st = tuple(chain(st[n], total[n], False) for n in range(NG))

        def forward(s, st):
            d, x, b, c, dst = ddec[s], dx[s], bb[rows(s), :], cb[rows(s), :], ds[s]
            acc, new = y[s], []
            for n in range(NG):
                p = jnp.exp2(d * r2[n]) * st[n]
                p_scr[s, n] = p
                h = p + x * wide(b[:, cols[n]])
                acc = acc + wide(c[:, cols[n]]) * h
                q[rows(s), cols[n]] = fold(dst * h)
                new.append(h)
            y[s] = acc
            return tuple(new)

        loop(forward, st)
        reduce(dc)

        def behind(k, A):
            s = S - 1 - k
            d, c, dst = ddec[s], cb[rows(s), :], ds[s]
            return tuple(
                jnp.exp2(d * r2[n]) * (dst * wide(c[:, cols[n]]) + A[n]) for n in range(NG)
            )

        A = loop(behind, zero)
        A = tuple(chain(A[n], total[n], True) for n in range(NG))

        def backward(k, carry):
            A, dr = carry
            s = S - 1 - k
            d, x, b, c, dst = ddec[s], dx[s], bb[rows(s), :], cb[rows(s), :], ds[s]
            ga, fa, nA, ndr = gb[s], fr[s], [], []
            for n in range(NG):
                G = dst * wide(c[:, cols[n]]) + A[n]
                nA.append(jnp.exp2(d * r2[n]) * G)
                flow = G * p_scr[s, n]
                ndr.append(dr[n] + flow * d)
                fa = fa + flow * rt[n]
                ga = ga + G * wide(b[:, cols[n]])
                q[rows(s), cols[n]] = fold(G * x)
            gb[s] = ga
            fr[s] = fa
            return tuple(nA), tuple(ndr)

        A, dr = loop(backward, (A, zero))
        reduce(db)
        for n in range(NG):
            drate[pl.ds(g * NG + n, 1), :] = jnp.sum(dr[n], axis=0, keepdims=True)
        return 0

    lax.fori_loop(0, NN // NG, group, 0)
    copies = []
    for a, (src, dst) in enumerate(((y, y_h), (gb, gb_h), (fr, fr_h))):
        for c in range(CHUNKS):
            copies.append(
                pltpu.make_async_copy(src.at[:, c, :], dst.at[pl.ds(c * S, S), :], sems.at[a, c])
            )
    for cp in copies:
        cp.start()
    for cp in copies:
        cp.wait()


def scan_both(ddec, dx, ds, bc, rate, NG=4):
    T, E = ddec.shape
    N = rate.shape[0]
    S = T // CHUNKS
    act = pltpu.VMEM((S, CHUNKS, E), f32)
    return pl.pallas_call(
        functools.partial(scan_kernel, S, NG),
        in_specs=[HBM] * 3 + [VMEM] * 3,
        out_specs=[HBM] * 3 + [VMEM] * 3,
        out_shape=[sds((T, E), f32)] * 3 + [sds((T, 128), f32)] * 2 + [sds((N, E), f32)],
        scratch_shapes=[act] * 6
        + [pltpu.VMEM((S, NG, CHUNKS, E), f32)]
        + [pltpu.VMEM((T, NG * 128), f32)] * 3
        + [pltpu.SemaphoreType.DMA((3, CHUNKS))],
        compiler_params=pltpu.CompilerParams(vmem_limit_bytes=60 << 20),
        cost_estimate=cost(60 * T * E * N, 24 * T * E, 4 * T * E * N),
        name="scan_both",
    )(ddec, dx, ds, bc, rate * LOG2E, rate)


def inter(v):
    return v.reshape((CHUNKS, v.shape[0] // CHUNKS) + v.shape[1:]).swapaxes(0, 1).reshape(v.shape)


def natural(v):
    return v.reshape((v.shape[0] // CHUNKS, CHUNKS) + v.shape[1:]).swapaxes(0, 1).reshape(v.shape)


def token_layout(lens, count):
    places = jnp.arange(count)
    begins = jnp.zeros_like(places)
    end = jnp.int32(0)
    for k in range(lens.shape[0]):
        start_of_padding = end
        end = end + lens[k]
        begins = begins + jnp.where(end <= places, lens[k], 0)
    return places - begins, (places < start_of_padding).astype(f32)


def lagged(values, lag):
    if lag == 0:
        return values
    return jnp.concatenate(
        [jnp.zeros((lag,) + values.shape[1:], values.dtype), values[: values.shape[0] - lag]], axis=0
    )


def leading(values, lag):
    if lag == 0:
        return values
    return jnp.concatenate(
        [values[lag:], jnp.zeros((lag,) + values.shape[1:], values.dtype)], axis=0
    )


def shards(
    hidden, out_grad, modality, lengths, in_weight, x_weight, dt_weight, out_weight,
    conv_weight, conv_bias, a_log, d_skip, dt_bias, norm_gain
):
    micro, rows, width = hidden.shape
    group = modality.shape[1]
    inner = conv_bias.shape[0]
    nstate = a_log.shape[0]
    taps = conv_weight.shape[0]
    kinds_all = modality[:, ::MBLK]
    plan = wgrad_plan(kinds_all)
    gain = lax.all_gather(norm_gain, "chan", axis=0, tiled=True)
    rate = -jnp.exp(a_log)
    x_small = jnp.swapaxes(x_weight, 1, 2)
    cols = x_small.shape[1]
    small = lax.all_gather(
        jnp.concatenate([x_small, dt_weight], axis=1), "seq", axis=0, tiled=False
    )
    small = jnp.swapaxes(small, 0, 1)
    x_full = small[:, :, :cols].reshape(MODES, -1, inner)
    dt_full = small[:, :, cols:].reshape(MODES, -1, inner)
    rank = dt_full.shape[1]
    scales, units, normed, gathered, ups = [], [], [], [], []
    for i in range(micro):
        source = hidden[i].astype(f32)
        scale = lax.rsqrt(jnp.mean(source * source, axis=1, keepdims=True) + 1e-05)
        unit = source * scale
        normed.append((unit * gain[None, :]).astype(bf16))
        scales.append(scale)
        units.append(unit)
    in_full = lax.all_gather(
        in_weight.reshape(MODES, -1, 2 * inner), "seq", axis=1, tiled=True
    )
    out_full = lax.all_gather(out_weight, "seq", axis=2, tiled=True)
    for i in range(micro):
        gathered.append(lax.all_gather(normed[i], "chan", axis=0, tiled=True))
        ups.append(lax.all_gather(out_grad[i], "chan", axis=0, tiled=True))
    outputs, input_grads, ys, d_mixes, xcs, d_projs, lows, d_pres = [], [], [], [], [], [], [], []
    sums = []
    g_gain = jnp.zeros((width,), f32)
    for i in range(micro):
        kinds = kinds_all[i]
        position, valid = token_layout(lengths[i, 0], group)
        keep = (position > 0)[:, None]
        valid = valid[:, None]
        reach = [(position >= lag).astype(f32)[:, None] for lag in range(taps)]
        mixed = gmm(kinds, gathered[i], in_full, False, f32, "in_proj")
        x_in, gate_in = mixed[:, :inner], mixed[:, inner:]
        conv = jnp.zeros_like(x_in) + conv_bias[None, :]
        for lag in range(taps):
            conv = conv + conv_weight[lag][None, :] * lagged(x_in, lag) * reach[lag]
        xc = jax.nn.silu(conv).astype(bf16)
        xc_f = xc.astype(f32)
        proj = lax.psum(gmm(kinds, xc, x_full, True, f32, "x_proj"), "chan")
        dt_low = proj[:, :rank].astype(bf16)
        bc = proj[:, rank:]
        dt_pre = gmm(kinds, dt_low, dt_full, False, f32, "dt_proj") + dt_bias[None, :]
        delta = jax.nn.softplus(dt_pre)
        d_y = gmm(kinds, ups[i], out_full, True, f32, "out_dgrad")
        gate = jax.nn.silu(gate_in)
        d_state = d_y * gate * valid
        dx = delta * xc_f
        ddec = jnp.where(keep, delta, RESET)
        s_y, s_gb, s_fr, s_b, s_c, s_rate = scan_both(ddec, dx, d_state, inter(bc), rate)
        scanned = s_y + d_skip[None, :] * xc_f
        y_out = (scanned * gate * valid).astype(bf16)
        branch = lax.psum_scatter(
            gmm(kinds, y_out, out_full, False, bf16, "out_proj"),
            "chan", scatter_dimension=0, tiled=True,
        )
        outputs.append((hidden[i].astype(f32) + branch.astype(f32)).astype(bf16))
        d_gate = (d_y * scanned * valid * dsilu(gate_in)).astype(bf16)
        d_delta = xc_f * s_gb + s_fr
        d_pre = (d_delta * jax.nn.sigmoid(dt_pre)).astype(bf16)
        d_low = gmm(kinds, d_pre, dt_full, True, f32, "dt_dgrad")
        d_bc = natural(jnp.concatenate([s_b[:, :nstate], s_c[:, :nstate]], axis=1))
        d_proj = lax.psum(jnp.concatenate([d_low, d_bc], axis=1), "chan").astype(bf16)
        d_xc = (
            d_state * d_skip[None, :]
            + delta * s_gb
            + gmm(kinds, d_proj, x_full, False, f32, "x_dgrad")
        )
        d_conv = d_xc * dsilu(conv)
        d_in = jnp.zeros_like(d_conv)
        conv_rows = []
        for lag in range(taps):
            masked = d_conv * reach[lag]
            conv_rows.append(jnp.sum(masked * lagged(x_in, lag), axis=0))
            d_in = d_in + conv_weight[lag][None, :] * leading(masked, lag)
        d_mixed = jnp.concatenate([d_in.astype(bf16), d_gate], axis=1)
        d_normed = lax.psum_scatter(
            gmm(kinds, d_mixed, in_full, True, bf16, "in_dgrad"),
            "chan", scatter_dimension=0, tiled=True,
        ).astype(f32)
        g_gain = g_gain + jnp.sum(d_normed * units[i], axis=0)
        d_unit = d_normed * gain[None, :]
        input_grads.append(
            scales[i] * (d_unit - units[i] * jnp.mean(d_unit * units[i], axis=1, keepdims=True))
            + out_grad[i].astype(f32)
        )
        ys.append(y_out)
        d_mixes.append(d_mixed)
        xcs.append(xc)
        d_projs.append(d_proj)
        lows.append(dt_low)
        d_pres.append(d_pre)
        sums.append(
            (
                jnp.stack(conv_rows, axis=0),
                jnp.sum(d_conv, axis=0),
                s_rate * rate,
                jnp.sum(d_state * xc_f, axis=0),
                jnp.sum(d_pre.astype(f32), axis=0),
            )
        )
    g_out = wgrad(plan, ys, ups, "out_wgrad", 256)
    g_dt = wgrad(plan, lows, d_pres, "dt_wgrad", 128)
    g_x = wgrad(plan, d_projs, xcs, "x_wgrad", d_projs[0].shape[1])
    g_in = wgrad(plan, gathered, d_mixes, "in_wgrad", 256)
    g_out = lax.psum_scatter(g_out, "seq", scatter_dimension=2, tiled=True)
    g_x = lax.psum_scatter(g_x, "seq", scatter_dimension=1, tiled=True)
    g_dt = lax.psum_scatter(g_dt, "seq", scatter_dimension=1, tiled=True)
    g_in = lax.psum_scatter(g_in, "seq", scatter_dimension=1, tiled=True)
    gain_part = lax.psum_scatter(g_gain, "chan", scatter_dimension=0, tiled=True)
    total = [sum(s[j] for s in sums) for j in range(5)]
    conv_total, bias_total, rate_total, skip_total, dtb_total, gain_total = lax.psum(
        (*total, gain_part), "seq"
    )
    return (
        jnp.stack(outputs, axis=0),
        jnp.stack(input_grads, axis=0),
        g_in.astype(f32).reshape(in_weight.shape),
        jnp.swapaxes(g_x.astype(f32), 1, 2),
        g_dt.astype(f32),
        g_out.astype(f32),
        conv_total,
        bias_total,
        rate_total,
        skip_total,
        dtb_total,
        gain_total,
    )


def solution(mesh):
    act = P(None, ("seq", "chan"), None)
    weights = (P(None, "seq", None, "chan"), P(None, "chan", "seq"), P(None, "seq", "chan"), P(None, "chan", "seq"))
    vectors = (P(None, "chan"), P("chan"), P(None, "chan"), P("chan"), P("chan"), P("chan"))
    return jax.shard_map(
        shards,
        mesh=mesh,
        in_specs=(act, act, P(None, "seq"), P(None, "seq", None), *weights, *vectors),
        out_specs=(act, act, *weights, *vectors),
        check_vma=False,
    )
```

```python
import functools

import jax
import jax.numpy as jnp
from jax import lax
from jax.experimental import pallas as pl
from jax.experimental.pallas import tpu as pltpu
from jax.sharding import PartitionSpec as P

MODES = 3
MBLK = 1024
LOG2E = 1.4426950408889634
RESET = 1.0e4
CHUNKS = 8
UNROLL = 8
RB = 512

f32, bf16 = jnp.float32, jnp.bfloat16
HBM = pl.BlockSpec(memory_space=pl.ANY)
VMEM = pl.BlockSpec(memory_space=pltpu.VMEM)
MESH = pl.DeviceIdType.MESH


def sds(shape, dtype):
    return jax.ShapeDtypeStruct(shape, dtype)


def cost(flops, nbytes, trans=0):
    return pl.CostEstimate(flops=int(flops), bytes_accessed=int(nbytes), transcendentals=int(trans))


def busy(us, nbytes):
    return cost(us * 1.1e9, nbytes)


def dsilu(value):
    sig = jax.nn.sigmoid(value)
    return sig * (1.0 + value * (1.0 - sig))


def by_tile(lefts, rights, left_dim):
    out = []
    for left, right in zip(lefts, rights):
        for t in range(right.shape[0] // MBLK):
            a = lax.slice_in_dim(left, t * MBLK, t * MBLK + MBLK, axis=left_dim)
            b = lax.slice_in_dim(right, t * MBLK, t * MBLK + MBLK, axis=0)
            dims = (((left_dim,), (0,)), ((), ()))
            out.append(lax.dot_general(a, b, dims, preferred_element_type=f32).astype(bf16))
    return out


def by_modality(kinds, tiles):
    out = []
    for m in range(MODES):
        out.append(
            sum(jnp.where(kinds[t] == m, tile.astype(f32), 0.0) for t, tile in enumerate(tiles)).astype(bf16)
        )
    return jnp.stack(out)


def by_modality_blocks(kinds, tiles, dim, n):
    blocks = [jnp.split(tile, n, axis=dim) for tile in tiles]
    return [by_modality(kinds, [b[j] for b in blocks]) for j in range(n)]


def chain(ends, total, back):
    row = lax.broadcasted_iota(jnp.int32, ends.shape, 0)
    for k in (1, 2, 4):
        shift = CHUNKS - k if back else k
        ok = (row < CHUNKS - k) if back else (row >= k)
        ends = ends + total * jnp.where(ok, pltpu.roll(ends, shift, 0), 0.0)
        total = total * jnp.where(ok, pltpu.roll(total, shift, 0), 1.0)
    shift = CHUNKS - 1 if back else 1
    ok = (row < CHUNKS - 1) if back else (row >= 1)
    return jnp.where(ok, pltpu.roll(ends, shift, 0), 0.0)


def scan_kernel(
    S, NG, ddec_h, dx_h, ds_h, bc_h, rate2, rate, y_h, gb_h, fr_h, dbc_h, drate,
    ddec, dx, ds, bc, y, gb, fr, dbc, p_scr, bb, cb, q, sems
):
    NN, L = rate.shape
    KT = L // 128
    copies = []
    for a, (src, dst) in enumerate(((ddec_h, ddec), (dx_h, dx), (ds_h, ds), (bc_h, bc))):
        for c in range(CHUNKS):
            copies.append(
                pltpu.make_async_copy(src.at[pl.ds(c * S, S), :], dst.at[:, c, :], sems.at[a, c])
            )
    for cp in copies:
        cp.start()
    dbc[...] = jnp.zeros_like(dbc)
    y[...] = jnp.zeros_like(y)
    gb[...] = jnp.zeros_like(gb)
    fr[...] = jnp.zeros_like(fr)
    for cp in copies:
        cp.wait()

    def rows(s):
        return pl.ds(pl.multiple_of(s * 8, 8), 8)

    def wide(v):
        return jnp.concatenate([v] * KT, axis=1)

    def fold(v):
        return sum(v[:, 128 * i : 128 * i + 128] for i in range(KT))

    def loop(body, init):
        def outer(k, carry):
            for u in range(UNROLL):
                carry = body(k * UNROLL + u, carry)
            return carry

        return lax.fori_loop(0, S // UNROLL, outer, init)

    dsum = lax.fori_loop(0, S, lambda s, a: a + ddec[s], jnp.zeros((8, L), f32))

    def group(g, _):
        kk = lax.broadcasted_iota(jnp.int32, (2 * NN, NG * 128), 0)
        ln = lax.broadcasted_iota(jnp.int32, (2 * NN, NG * 128), 1) // 128
        Xb = jnp.where(kk == g * NG + ln, 1.0, 0.0).astype(bf16)
        Xc = jnp.where(kk == NN + g * NG + ln, 1.0, 0.0).astype(bf16)
        rr = lax.broadcasted_iota(jnp.int32, (NG * 128, 128), 0) // 128
        cc = lax.broadcasted_iota(jnp.int32, (NG * 128, 128), 1)
        Rb = jnp.where(cc == rr + g * NG, 1.0, 0.0).astype(bf16)
        Rc = jnp.where(cc == rr + NN + g * NG, 1.0, 0.0).astype(bf16)

        v = bc[...].reshape(S * CHUNKS, 128)[:, : 2 * NN]
        hi = v.astype(bf16)
        lo = (v - hi.astype(f32)).astype(bf16)
        bb[...] = dot(hi, Xb) + dot(lo, Xb)
        cb[...] = dot(hi, Xc) + dot(lo, Xc)

        def reduce(R):
            out = dot(q[...].astype(bf16), R)
            dbc[...] += out.reshape(S, CHUNKS, 128)

        r2 = [jnp.broadcast_to(rate2[pl.ds(g * NG + n, 1), :], (8, L)) for n in range(NG)]
        rt = [jnp.broadcast_to(rate[pl.ds(g * NG + n, 1), :], (8, L)) for n in range(NG)]
        total = [jnp.exp2(dsum * r2[n]) for n in range(NG)]
        zero = tuple(jnp.zeros((8, L), f32) for _ in range(NG))
        cols = [slice(128 * n, 128 * n + 128) for n in range(NG)]

        def ahead(s, st):
            d, x, b = ddec[s], dx[s], bb[rows(s), :]
            return tuple(
                jnp.exp2(d * r2[n]) * st[n] + x * wide(b[:, cols[n]]) for n in range(NG)
            )

        st = loop(ahead, zero)
        st = tuple(chain(st[n], total[n], False) for n in range(NG))

        def forward(s, st):
            d, x, b, c, dst = ddec[s], dx[s], bb[rows(s), :], cb[rows(s), :], ds[s]
            acc, new = y[s], []
            for n in range(NG):
                p = jnp.exp2(d * r2[n]) * st[n]
                p_scr[s, n] = p
                h = p + x * wide(b[:, cols[n]])
                acc = acc + wide(c[:, cols[n]]) * h
                q[rows(s), cols[n]] = fold(dst * h)
                new.append(h)
            y[s] = acc
            return tuple(new)

        loop(forward, st)
        reduce(Rc)

        def behind(k, A):
            s = S - 1 - k
            d, c, dst = ddec[s], cb[rows(s), :], ds[s]
            return tuple(
                jnp.exp2(d * r2[n]) * (dst * wide(c[:, cols[n]]) + A[n]) for n in range(NG)
            )

        A = loop(behind, zero)
        A = tuple(chain(A[n], total[n], True) for n in range(NG))

        def backward(k, carry):
            A, dr = carry
            s = S - 1 - k
            d, x, b, c, dst = ddec[s], dx[s], bb[rows(s), :], cb[rows(s), :], ds[s]
            ga, fa, nA, ndr = gb[s], fr[s], [], []
            for n in range(NG):
                G = dst * wide(c[:, cols[n]]) + A[n]
                nA.append(jnp.exp2(d * r2[n]) * G)
                flow = G * p_scr[s, n]
                ndr.append(dr[n] + flow * d)
                fa = fa + flow * rt[n]
                ga = ga + G * wide(b[:, cols[n]])
                q[rows(s), cols[n]] = fold(G * x)
            gb[s] = ga
            fr[s] = fa
            return tuple(nA), tuple(ndr)

        A, dr = loop(backward, (A, zero))
        reduce(Rb)
        for n in range(NG):
            drate[pl.ds(g * NG + n, 1), :] = jnp.sum(dr[n], axis=0, keepdims=True)
        return 0

    lax.fori_loop(0, NN // NG, group, 0)
    copies = []
    for a, (src, dst) in enumerate(((y, y_h), (gb, gb_h), (fr, fr_h), (dbc, dbc_h))):
        for c in range(CHUNKS):
            copies.append(
                pltpu.make_async_copy(src.at[:, c, :], dst.at[pl.ds(c * S, S), :], sems.at[a, c])
            )
    for cp in copies:
        cp.start()
    for cp in copies:
        cp.wait()


def scan_both(ddec, dx, ds, bc, rate, NG=4):
    T, E = ddec.shape
    N = rate.shape[0]
    S = T // CHUNKS
    act = pltpu.VMEM((S, CHUNKS, E), f32)
    thin = pltpu.VMEM((S, CHUNKS, 128), f32)
    return pl.pallas_call(
        functools.partial(scan_kernel, S, NG),
        in_specs=[HBM] * 4 + [VMEM] * 2,
        out_specs=[HBM] * 4 + [VMEM],
        out_shape=[sds((T, E), f32)] * 3 + [sds((T, 128), f32), sds((N, E), f32)],
        scratch_shapes=[act] * 3 + [thin] + [act] * 3 + [thin]
        + [pltpu.VMEM((S, NG, CHUNKS, E), f32)]
        + [pltpu.VMEM((T, NG * 128), f32)] * 3
        + [pltpu.SemaphoreType.DMA((4, CHUNKS))],
        compiler_params=pltpu.CompilerParams(vmem_limit_bytes=60 << 20),
        cost_estimate=busy(105.0 * T * E * N / (2048 * 512 * 16), 24 * T * E),
        name="scan_both",
    )(ddec, dx, ds, bc, rate * LOG2E, rate)


def sum_kernel(pairs, n, *refs):
    parts, outs, rest = refs[:n], refs[n : 2 * n], refs[2 * n :]
    half, near, mine, far = rest[:n], rest[n : 2 * n], rest[2 * n : 3 * n], rest[3 * n : 4 * n]
    sems_s, sems_r = rest[4 * n :]
    T = parts[0].shape[1]
    H = T // 2
    Q = H // pairs
    me = lax.axis_index("chan")
    core, z = lax.rem(me, 2), me // 2
    mate = me + 1 - 2 * core
    peers = [lax.rem(z + k, pairs) for k in range(1, pairs)]
    gate = pltpu.get_barrier_semaphore()
    for dev in [mate] + [2 * p + core for p in peers]:
        pl.semaphore_signal(gate, inc=1, device_id={"chan": dev}, device_id_type=MESH)
    pl.semaphore_wait(gate, pairs)

    def cols(i, n):
        return pl.ds(pl.multiple_of(i * n, n), n)

    def send(a, src, dst, k, dev):
        c = pltpu.make_async_remote_copy(
            src_ref=src, dst_ref=dst, send_sem=sems_s.at[a, k], recv_sem=sems_r.at[a, k],
            device_id={"chan": dev}, device_id_type=MESH,
        )
        c.start()
        return c

    first = [send(a, parts[a].at[:, cols(1 - core, H)], near[a], 0, mate) for a in range(n)]
    for a in range(n):
        first[a].wait()
        half[a][...] = (
            parts[a][:, cols(core, H)].astype(f32) + near[a][...].astype(f32)
        ).astype(half[a].dtype)
    sends = [
        [send(a, half[a].at[:, cols(p, Q)], far[a].at[k], 1 + k, 2 * p + core) for a in range(n)]
        for k, p in enumerate(peers)
    ]
    totals = [half[a][:, cols(z, Q)].astype(f32) for a in range(n)]
    for k in range(pairs - 1):
        for a in range(n):
            sends[k][a].wait()
            totals[a] = totals[a] + far[a][k].astype(f32)
    at = pl.ds(pl.multiple_of(core * H + z * Q, Q), Q)
    sends = []
    for a in range(n):
        mine[a][...] = totals[a].astype(mine[a].dtype)
        for k, p in enumerate(peers):
            sends.append(send(a, mine[a], outs[a].at[:, at], pairs + k, 2 * p + core))
        outs[a][:, at] = mine[a][...]
    for c in sends:
        c.wait()
    last = [
        send(a, outs[a].at[:, cols(core, H)], outs[a].at[:, cols(core, H)], 2 * pairs - 1, mate)
        for a in range(n)
    ]
    for c in last:
        c.wait()


def chan_sum(parts, number):
    n = len(parts)
    T = parts[0].shape[1]
    pairs = lax.axis_size("chan") // 2
    Q = T // 2 // pairs
    if Q % 128:
        return [lax.psum(p.astype(f32), "chan").astype(p.dtype) for p in parts]
    shapes = [(p.shape[0], p.dtype) for p in parts]
    return pl.pallas_call(
        functools.partial(sum_kernel, pairs, n),
        in_specs=[VMEM] * n,
        out_specs=[VMEM] * n,
        out_shape=[sds(p.shape, p.dtype) for p in parts],
        scratch_shapes=[pltpu.VMEM((c, T // 2), d) for c, d in shapes] * 2
        + [pltpu.VMEM((c, Q), d) for c, d in shapes]
        + [pltpu.VMEM((pairs - 1, c, Q), d) for c, d in shapes]
        + [pltpu.SemaphoreType.DMA((n, 2 * pairs))] * 2,
        compiler_params=pltpu.CompilerParams(
            collective_id=number, has_side_effects=True, vmem_limit_bytes=32 << 20
        ),
        cost_estimate=busy(26.0, 4 * T),
        name="chan_sum",
    )(*parts)


def places(lens, block):
    t = lax.broadcasted_iota(jnp.int32, (RB, 1), 0) + block * RB
    begins = jnp.zeros_like(t)
    end = jnp.int32(0)
    start_of_padding = end
    for k in range(lens.shape[0]):
        start_of_padding = end
        end = end + lens[k]
        begins = begins + jnp.where(end <= t, lens[k], 0)
    return t - begins, jnp.where(t < start_of_padding, 1.0, 0.0)


def silu(v):
    return v * jax.nn.sigmoid(v)


def dot(a, b):
    return jnp.dot(a, b, preferred_element_type=f32)


def dot_nt(a, b):
    return lax.dot_general(a, b, (((1,), (1,)), ((), ())), preferred_element_type=f32)


def dot_tn(a, b):
    return lax.dot_general(a, b, (((0,), (0,)), ((), ())), preferred_element_type=f32)


def conv_of(xe, cw, cb, position, taps):
    conv = jnp.zeros((RB, cw.shape[1]), f32) + cb[...]
    lags = []
    for k in range(taps):
        lag = xe[pl.ds(8 - k, RB), :]
        lags.append(lag)
        conv = conv + cw[k : k + 1, :] * lag * jnp.where(position >= k, 1.0, 0.0)
    return conv, lags


def in_kernel(taps, kinds, lens, g, xw, cw, cb, *rest):
    ws, (x_o, gate_o, xc_o, low_o, thin_o, xe) = rest[:-6], rest[-6:]
    blk = pl.program_id(0)
    P4 = ws[0].shape[1]
    inner = cw.shape[1]
    mixed = sum(dot(g[:, P4 * j : P4 * j + P4], w[0]) for j, w in enumerate(ws))
    x = mixed[:, :inner]
    x_o[...] = x
    gate_o[...] = mixed[:, inner:]

    @pl.when(blk == 0)
    def _():
        xe[pl.ds(0, 8), :] = jnp.zeros((8, inner), f32)

    @pl.when(blk > 0)
    def _():
        xe[pl.ds(0, 8), :] = xe[pl.ds(RB, 8), :]

    xe[pl.ds(8, RB), :] = x
    position, valid = places(lens, blk)
    conv, lags = conv_of(xe, cw, cb, position, taps)
    xc = silu(conv).astype(bf16)
    xc_o[...] = xc
    part = dot_nt(xw[0], xc)
    rank = low_o.shape[0]
    low_o[...] = part[:rank].astype(bf16)
    thin_o[...] = part[rank:]


def mid_kernel(kinds, lens, u, gate, xc, low, thin, dtw, dtb, *rest):
    ws, (ddec_o, delta_o, dx_o, ds_o, dy_o, bc_o) = rest[:-6], rest[-6:]
    blk = pl.program_id(0)
    P4 = ws[0].shape[2]
    dy = sum(dot_nt(u[:, P4 * j : P4 * j + P4], w[0]) for j, w in enumerate(ws))
    position, valid = places(lens, blk)
    pre = dot_tn(low[...], dtw[0]) + dtb[...]
    delta = jnp.maximum(pre, 0.0) + jnp.log1p(jnp.exp(-jnp.abs(pre)))
    ddec_o[...] = jnp.where(position > 0, delta, RESET)
    delta_o[...] = delta
    dx_o[...] = delta * xc[...].astype(f32)
    ds_o[...] = dy * silu(gate[...]) * valid
    dy_o[...] = dy
    bc_o[...] = jnp.concatenate([thin[...], jnp.zeros((128 - thin.shape[0], RB), f32)], axis=0).T


def post_kernel(nbc, kinds, lens, y, gb, fr, ds, dy, gate, xc, delta, dbc, skip, dtw, *rest):
    ws, (out_o, y_o, dgate_o, dpre_o, dxc_o, dpp_o, sum_o) = rest[:-7], rest[-7:]
    blk = pl.program_id(0)
    position, valid = places(lens, blk)
    x = xc[...].astype(f32)
    z = gate[...]
    scanned = y[...] + skip[...] * x
    yo = (scanned * silu(z) * valid).astype(bf16)
    y_o[...] = yo
    dgate_o[...] = (dy[...] * scanned * valid * dsilu(z)).astype(bf16)
    dl = delta[...]
    g = gb[...]
    dpre = ((x * g + fr[...]) * (1.0 - jnp.exp(-dl))).astype(bf16)
    dpre_o[...] = dpre
    dlow = dot_nt(dtw[0], dpre)
    dpp_o[...] = jnp.concatenate([dlow, dbc[...].T[:nbc, :]], axis=0).astype(bf16)
    d = ds[...]
    dxc_o[...] = d * skip[...] + dl * g
    P4 = ws[0].shape[2]
    for j, w in enumerate(ws):
        out_o[:, P4 * j : P4 * j + P4] = dot(yo, w[0]).astype(bf16)

    @pl.when(blk == 0)
    def _():
        sum_o[...] = jnp.zeros_like(sum_o)

    sum_o[0:1, :] += jnp.sum(d * x, axis=0, keepdims=True)
    sum_o[1:2, :] += jnp.sum(dpre.astype(f32), axis=0, keepdims=True)


def back_kernel(taps, nblk, kinds, lens, dproj, xw, dxc, x, xprev, cw, cb, dgate, g, *rest):
    ws, (din_o, dn_o, sum_o, gain_o, xe, mk) = rest[:-6], rest[-6:]
    step = pl.program_id(0)
    blk = nblk - 1 - step
    inner = cw.shape[1]
    position, valid = places(lens, blk)
    xe[pl.ds(0, 8), :] = jnp.where(blk > 0, xprev[...], 0.0)
    xe[pl.ds(8, RB), :] = x[...]
    conv, lags = conv_of(xe, cw, cb, position, taps)
    dconv = (dxc[...] + dot_tn(dproj[...], xw[0])) * dsilu(conv)

    @pl.when(step == 0)
    def _():
        sum_o[...] = jnp.zeros_like(sum_o)
        gain_o[...] = jnp.zeros_like(gain_o)
        mk[:, pl.ds(RB, 8), :] = jnp.zeros((taps, 8, inner), f32)

    @pl.when(step > 0)
    def _():
        mk[:, pl.ds(RB, 8), :] = mk[:, pl.ds(0, 8), :]

    din = jnp.zeros((RB, inner), f32)
    for k in range(taps):
        masked = dconv * jnp.where(position >= k, 1.0, 0.0)
        mk[k, pl.ds(0, RB), :] = masked
        sum_o[k : k + 1, :] += jnp.sum(masked * lags[k], axis=0, keepdims=True)
        din = din + cw[k : k + 1, :] * mk[k, pl.ds(k, RB), :]
    sum_o[taps : taps + 1, :] += jnp.sum(dconv, axis=0, keepdims=True)
    din_o[...] = din.astype(bf16)
    dmix = jnp.concatenate([din.astype(bf16), dgate[...]], axis=1)
    P4 = ws[0].shape[1]
    for j, w in enumerate(ws):
        part = dot_nt(dmix, w[0])
        at = slice(P4 * j, P4 * j + P4)
        dn_o[:, at] = part.astype(bf16)
        gain_o[0:1, at] += jnp.sum(part * g[:, at].astype(f32), axis=0, keepdims=True)


def stage(kernel, name, T, blocked, weights, whole, outs, sums, scratch, kinds, lens, us, reverse=False, prev=None, order=None, across={}, out_across=()):
    n = T // RB
    at = (lambda b: n - 1 - b) if reverse else (lambda b: b)
    per = MBLK // RB
    row = lambda b, kinds, lens: (at(b), 0)
    const = lambda b, kinds, lens: (0, 0)
    specs = {}
    args = {}
    col = lambda b, kinds, lens: (0, at(b))
    for key, a in blocked.items():
        specs[key], args[key] = pl.BlockSpec((RB, a.shape[1]), row), a
    for key, a in across.items():
        specs[key], args[key] = pl.BlockSpec((a.shape[0], RB), col), a
    for key, a in weights.items():
        specs[key] = pl.BlockSpec((1,) + a.shape[1:], lambda b, kinds, lens: (kinds[at(b) // per], 0, 0))
        args[key] = a
    for key, a in whole.items():
        specs[key], args[key] = pl.BlockSpec(a.shape, const), a
    if prev is not None:
        key, a = prev
        specs[key] = pl.BlockSpec((8, a.shape[1]), lambda b, kinds, lens: (jnp.maximum(at(b) * (RB // 8) - 1, 0), 0))
        args[key] = a
    out_specs = [pl.BlockSpec((RB, c), row) for c, _ in outs] + [pl.BlockSpec((c, RB), col) for c, _ in out_across] + [pl.BlockSpec(shape, const) for shape in sums]
    out_shape = [sds((T, c), dtype) for c, dtype in outs] + [sds((c, T), dtype) for c, dtype in out_across] + [sds(shape, f32) for shape in sums]
    nbytes = sum(a.size * a.dtype.itemsize for a in blocked.values()) + sum(T * c * 4 for c, _ in outs)
    return pl.pallas_call(
        kernel,
        grid_spec=pltpu.PrefetchScalarGridSpec(
            num_scalar_prefetch=2,
            grid=(n,),
            in_specs=[specs[k] for k in order],
            out_specs=out_specs,
            scratch_shapes=scratch,
        ),
        out_shape=out_shape,
        compiler_params=pltpu.CompilerParams(vmem_limit_bytes=56 << 20),
        cost_estimate=busy(us, nbytes),
        name=name,
    )(kinds, lens, *[args[k] for k in order])


def swap(v, bits, axis="seq"):
    n = lax.axis_size(axis)
    return lax.ppermute(v, axis, [(i, i ^ bits) for i in range(n)])


def square_gather_near(own):
    n = lax.axis_size("seq")
    return [own] + [swap(own, j) for j in range(1, 3 if n == 4 else n)]


def square_gather_far(blocks):
    if lax.axis_size("seq") != 4:
        return blocks
    own, by_x, by_y = blocks
    half = own.shape[1] // 2
    first = swap(by_x[:, :half], 2)
    second = swap(by_y[:, half:], 1)
    return [own, by_x, by_y, jnp.concatenate([first, second], axis=1)]


def scatter_far(parts):
    if len(parts) != 4:
        return []
    half = parts[3].shape[1] // 2
    return [swap(parts[3][:, :half], 1), swap(parts[3][:, half:], 2)]


def scatter_near(parts, far):
    if len(parts) != 4:
        return [parts[0]] + [swap(p, j) for j, p in enumerate(parts) if j]
    own, for_x, for_y, _ = parts
    a, b = far
    half = a.shape[1]
    for_y = jnp.concatenate(
        [(for_y[:, :half].astype(f32) + a.astype(f32)).astype(bf16), for_y[:, half:]], axis=1
    )
    for_x = jnp.concatenate(
        [for_x[:, :half], (for_x[:, half:].astype(f32) + b.astype(f32)).astype(bf16)], axis=1
    )
    return [own, swap(for_x, 1), swap(for_y, 2)]


def total_of(terms):
    return sum(t.astype(f32) for t in terms)


def seq_sum(v):
    return v + sum(swap(v, j) for j in range(1, lax.axis_size("seq")))


def chan_scatter(v):
    me = lax.axis_index("chan")
    bit = lax.axis_size("chan") // 2
    while bit:
        low, high = jnp.split(v, 2, axis=1)
        up = (me & bit) > 0
        v = jnp.where(up, high, low) + swap(jnp.where(up, low, high), bit, "chan")
        bit //= 2
    return v


def square_order(v, me):
    n = lax.axis_size("seq")
    parts = jnp.split(v, n, axis=-1)
    bit = 1
    while bit < n:
        on = (me & bit) > 0
        parts = [jnp.where(on, parts[i ^ bit], parts[i]) for i in range(n)]
        bit *= 2
    return jnp.concatenate(parts, axis=-1)


def shards(
    hidden, out_grad, modality, lengths, in_weight, x_weight, dt_weight, out_weight,
    conv_weight, conv_bias, a_log, d_skip, dt_bias, norm_gain
):
    micro, rows, width = hidden.shape
    T = modality.shape[1]
    inner = conv_bias.shape[0]
    nstate = a_log.shape[0]
    taps = conv_weight.shape[0]
    me = lax.axis_index("seq")
    nseq = lax.axis_size("seq")
    kinds_all = modality[:, ::MBLK]
    flat = kinds_all.reshape(-1)
    rate = -jnp.exp(a_log)
    P4 = in_weight.shape[1]
    w_own, norm_gain = lax.optimization_barrier(
        (in_weight.reshape(MODES, P4, 2 * inner), norm_gain)
    )
    w_in = square_gather_near(w_own)
    gain = lax.all_gather(norm_gain, "chan", axis=0, tiled=True)
    x_small = jnp.swapaxes(x_weight, 1, 2)
    ncols = x_small.shape[1]
    scales, units, normed, flipped = [], [], [], []
    for i in range(micro):
        source = hidden[i].astype(f32)
        scale = lax.rsqrt(jnp.mean(source * source, axis=1, keepdims=True) + 1e-05)
        unit = source * scale
        normed.append(square_order((unit * gain[None, :]).astype(bf16), me))
        flipped.append(square_order(out_grad[i], me))
        scales.append(scale)
        units.append(unit)
    w_in = square_gather_far(w_in)
    small = jnp.concatenate([x_small, dt_weight], axis=1)
    small = jnp.concatenate([small] + [swap(small, b) for b in range(1, nseq)], axis=2)
    small = square_order(small, me)
    x_full = jnp.concatenate(jnp.split(small[:, :ncols], nseq, axis=2), axis=1)
    dt_full = jnp.concatenate(jnp.split(small[:, ncols:], nseq, axis=2), axis=1)
    rank = dt_full.shape[1]
    later, w_in[-1] = lax.optimization_barrier((out_weight, w_in[-1]))
    w_out = square_gather_near(later)
    gathered = [lax.all_gather(normed[i], "chan", axis=0, tiled=True) for i in range(micro)]
    ups = [lax.all_gather(flipped[i], "chan", axis=0, tiled=True) for i in range(micro)]
    win = {f"w{j}": w for j, w in enumerate(w_in)}
    ws = list(win)
    vec = dict(cw=conv_weight, cb=conv_bias[None, :])
    skip, dtb = d_skip[None, :], dt_bias[None, :]
    branches, dn_parts, sums = [], [], []
    t_out, t_gate, t_x, t_dt, t_xw, d_ins = [], [], [], [], [], []

    def finish(c, d_proj):
        i = c["i"]
        d_in, dn_part, sum_b, sum_g = stage(
            functools.partial(back_kernel, taps, T // RB), "back_stage", T,
            dict(dxc=c["dxc"], x=c["x"], dgate=c["dgate"], g=gathered[i]), dict(**win, xw=x_full), vec,
            [(inner, bf16), (width, bf16)], [(8, inner), (8, width)],
            [pltpu.VMEM((RB + 8, inner), f32), pltpu.VMEM((taps, RB + 8, inner), f32)],
            kinds_all[i], lengths[i, 0], 26.0,
            reverse=True, prev=("xprev", c["x"]),
            order=["dproj", "xw", "dxc", "x", "xprev", "cw", "cb", "dgate", "g", *ws],
            across=dict(dproj=d_proj),
        )
        d_ins.append(d_in)
        t_xw.extend(by_tile([d_proj], [c["xc"]], 1))
        sums.append((c["sum_a"], sum_b, c["s_rate"] * rate, sum_g[:1]))
        return dn_part

    carried = None
    for i in range(micro):
        kinds, lens = kinds_all[i], lengths[i, 0]
        if carried is not None:
            gathered[i], d_part = lax.optimization_barrier((gathered[i], d_part))
        x_in, gate, xc, low_part, bc_part = stage(
            functools.partial(in_kernel, taps), "in_stage", T,
            dict(g=gathered[i]), dict(**win, xw=x_full), vec,
            [(inner, f32), (inner, f32), (inner, bf16)], [],
            [pltpu.VMEM((RB + 8, inner), f32)], kinds, lens, 21.0,
            order=["g", "xw", "cw", "cb", *ws],
            out_across=((rank, bf16), (2 * nstate, f32)),
        )
        if carried is None:
            *w_out, bc_part = lax.optimization_barrier((*w_out, bc_part))
            wout = {f"w{j}": w for j, w in enumerate(square_gather_far(w_out))}
            low, thin = chan_sum([low_part, bc_part], 0)
        else:
            low, thin, d_proj = chan_sum([low_part, bc_part, d_part], 1)
            dn_part = finish(carried, d_proj)
            thin, dn_part = lax.optimization_barrier((thin, dn_part))
            dn_parts.append(lax.psum_scatter(dn_part, "chan", scatter_dimension=0, tiled=True))
        ddec, delta, dx, ds, dy, bc = stage(
            mid_kernel, "mid_stage", T,
            dict(u=ups[i], gate=gate, xc=xc), dict(**wout, dtw=dt_full), dict(dtb=dtb),
            [(inner, f32)] * 5 + [(128, f32)], [], [], kinds, lens, 19.0,
            order=["u", "gate", "xc", "low", "thin", "dtw", "dtb", *ws], across=dict(low=low, thin=thin),
        )
        y, gb, fr, dbc, s_rate = scan_both(ddec, dx, ds, bc, rate)
        if dn_parts:
            dbc, branches, dn_parts = lax.optimization_barrier((dbc, branches, dn_parts))
        out_part, y_out, d_gate, d_pre, dxc, d_part, sum_a = stage(
            functools.partial(post_kernel, 2 * nstate), "post_stage", T,
            dict(y=y, gb=gb, fr=fr, ds=ds, dy=dy, gate=gate, xc=xc, delta=delta, dbc=dbc),
            dict(**wout, dtw=dt_full), dict(skip=skip),
            [(width, bf16), (inner, bf16), (inner, bf16), (inner, bf16), (inner, f32)],
            [(8, inner)], [], kinds, lens, 23.0,
            order=["y", "gb", "fr", "ds", "dy", "gate", "xc", "delta", "dbc", "skip", "dtw", *ws],
            out_across=((x_full.shape[1], bf16),),
        )
        branches.append(lax.psum_scatter(out_part, "chan", scatter_dimension=0, tiled=True))
        t_out += by_tile([y_out], [ups[i]], 0)
        t_gate += by_tile([gathered[i]], [d_gate], 0)
        t_dt += by_tile([low], [d_pre], 1)
        carried = dict(i=i, dxc=dxc, x=x_in, dgate=d_gate, xc=xc, sum_a=sum_a, s_rate=s_rate)
    g_out = by_modality_blocks(flat, t_out, 1, nseq)
    g_gate = by_modality_blocks(flat, t_gate, 0, nseq)
    far = scatter_far(g_out)
    d_part, far, g_gate[-1] = lax.optimization_barrier((d_part, far, g_gate[-1]))
    g_out = scatter_near(g_out, far)
    (d_proj,) = chan_sum([d_part], 2)
    far = scatter_far(g_gate)
    d_proj, far, g_out = lax.optimization_barrier((d_proj, far, g_out))
    g_gate = scatter_near(g_gate, far)
    dn_part = finish(carried, d_proj)
    dn_part, branches[-1] = lax.optimization_barrier((dn_part, branches[-1]))
    dn_parts.append(lax.psum_scatter(dn_part, "chan", scatter_dimension=0, tiled=True))
    g_dt = by_modality(flat, t_dt)
    g_xw = by_modality(flat, t_xw)
    ndt = dt_weight.shape[1]

    def seat_rows(bits):
        seat = me ^ bits
        a = lax.dynamic_slice_in_dim(g_xw, seat * ncols, ncols, 1)
        b = lax.dynamic_slice_in_dim(g_dt, seat * ndt, ndt, 1)
        return jnp.concatenate([a, b], axis=1)

    g_small = [seat_rows(0)] + [swap(seat_rows(b), b) for b in range(1, nseq)]
    totals = [sum(s[j] for s in sums) for j in range(4)]
    gain_rows = square_order(totals[3], me).reshape(-1, inner)
    vectors = seq_sum(jnp.concatenate([*totals[:3], gain_rows], axis=0))
    gain_total = chan_scatter(vectors[-gain_rows.shape[0] :].reshape(1, width))[0] / norm_gain
    last_in, g_gate, vectors, g_small = lax.optimization_barrier((d_ins[-1], g_gate, vectors, g_small))
    for i in range(micro):
        t_x += by_tile([gathered[i]], [last_in if i == micro - 1 else d_ins[i]], 0)
    g_x = by_modality_blocks(flat, t_x, 0, nseq)
    g_x = scatter_near(g_x, scatter_far(g_x))
    g_out, g_gate, g_x = total_of(g_out), total_of(g_gate), total_of(g_x)
    outputs, input_grads = [], []
    for i in range(micro):
        branch = square_order(branches[i].astype(f32), me)
        outputs.append((hidden[i].astype(f32) + branch).astype(bf16))
        d_unit = square_order(dn_parts[i].astype(f32), me) * gain[None, :]
        input_grads.append(
            scales[i] * (d_unit - units[i] * jnp.mean(d_unit * units[i], axis=1, keepdims=True))
            + out_grad[i].astype(f32)
        )
    g_small = total_of(g_small)
    return (
        jnp.stack(outputs, axis=0),
        jnp.stack(input_grads, axis=0),
        jnp.stack([g_x, g_gate], axis=2),
        jnp.swapaxes(g_small[:, :ncols], 1, 2),
        g_small[:, ncols:],
        g_out,
        vectors[8 : 8 + taps],
        vectors[8 + taps],
        vectors[16 : 16 + nstate],
        vectors[0],
        vectors[1],
        gain_total,
    )


def solution(mesh):
    act = P(None, ("seq", "chan"), None)
    weights = (P(None, "seq", None, "chan"), P(None, "chan", "seq"), P(None, "seq", "chan"), P(None, "chan", "seq"))
    vectors = (P(None, "chan"), P("chan"), P(None, "chan"), P("chan"), P("chan"), P("chan"))
    return jax.shard_map(
        shards,
        mesh=mesh,
        in_specs=(act, act, P(None, "seq"), P(None, "seq", None), *weights, *vectors),
        out_specs=(act, act, *weights, *vectors),
        check_vma=False,
    )
```

```python
import functools

import jax
import jax.numpy as jnp
from jax import lax
from jax.experimental import pallas as pl
from jax.experimental.pallas import tpu as pltpu
from jax.sharding import PartitionSpec as P

MODES = 3
MBLK = 1024
LOG2E = 1.4426950408889634
RESET = 1.0e4
CHUNKS = 8
UNROLL = 8
EARLY = 0.2
RB = 512

f32, bf16 = jnp.float32, jnp.bfloat16
HBM = pl.BlockSpec(memory_space=pl.ANY)
VMEM = pl.BlockSpec(memory_space=pltpu.VMEM)
MESH = pl.DeviceIdType.MESH


def sds(shape, dtype):
    return jax.ShapeDtypeStruct(shape, dtype)


def cost(flops, nbytes, trans=0):
    return pl.CostEstimate(flops=int(flops), bytes_accessed=int(nbytes), transcendentals=int(trans))


def busy(us, nbytes):
    return cost(us * EARLY * 1.1e9, nbytes * EARLY)


def dsilu(value):
    sig = jax.nn.sigmoid(value)
    return sig * (1.0 + value * (1.0 - sig))


def by_tile(lefts, rights, left_dim, dtype=bf16):
    out = []
    for left, right in zip(lefts, rights):
        for t in range(right.shape[0] // MBLK):
            a = lax.slice_in_dim(left, t * MBLK, t * MBLK + MBLK, axis=left_dim)
            b = lax.slice_in_dim(right, t * MBLK, t * MBLK + MBLK, axis=0)
            dims = (((left_dim,), (0,)), ((), ()))
            out.append(lax.dot_general(a, b, dims, preferred_element_type=f32).astype(dtype))
    return out


def by_modality(kinds, tiles):
    out = []
    for m in range(MODES):
        out.append(
            sum(jnp.where(kinds[t] == m, tile.astype(f32), 0.0) for t, tile in enumerate(tiles)).astype(bf16)
        )
    return jnp.stack(out)


def by_modality_blocks(kinds, tiles, dim, n):
    blocks = [jnp.split(tile, n, axis=dim) for tile in tiles]
    return [by_modality(kinds, [b[j] for b in blocks]) for j in range(n)]


def chain(ends, total, back):
    row = lax.broadcasted_iota(jnp.int32, ends.shape, 0)
    for k in (1, 2, 4):
        shift = CHUNKS - k if back else k
        ok = (row < CHUNKS - k) if back else (row >= k)
        ends = ends + total * jnp.where(ok, pltpu.roll(ends, shift, 0), 0.0)
        total = total * jnp.where(ok, pltpu.roll(total, shift, 0), 1.0)
    shift = CHUNKS - 1 if back else 1
    ok = (row < CHUNKS - 1) if back else (row >= 1)
    return jnp.where(ok, pltpu.roll(ends, shift, 0), 0.0)


def scan_kernel(S, NG, mode, *refs):
    ahead_too, back_too = mode != 2, mode != 1
    ins, refs = refs[:4], refs[4:]
    rate2, rate, refs = refs[0], refs[1], refs[2:]
    kept_h = None
    if mode == 2:
        kept_h, refs = refs[0], refs[1:]
    y_h = gb_h = fr_h = drate = y = gb = fr = None
    if ahead_too:
        y_h, refs = refs[0], refs[1:]
    if back_too:
        gb_h, fr_h, drate, refs = refs[0], refs[1], refs[2], refs[3:]
    dbc_h, refs = refs[0], refs[1:]
    if mode == 1:
        kept_h, refs = refs[0], refs[1:]
    ddec, dx, ds, bc, dbc, p_scr, bb, cb, q, sems, kept_sem = refs[:11]
    refs = refs[11:]
    if ahead_too:
        y, refs = refs[0], refs[1:]
    if back_too:
        gb, fr = refs
    NN, L = rate.shape
    KT = L // 128
    groups = NN // NG
    copies = []
    for a, (src, dst) in enumerate(zip(ins, (ddec, dx, ds, bc))):
        for c in range(CHUNKS):
            copies.append(
                pltpu.make_async_copy(src.at[pl.ds(c * S, S), :], dst.at[:, c, :], sems.at[a, c])
            )
    for cp in copies:
        cp.start()
    if mode == 2:
        pltpu.make_async_copy(kept_h.at[0], p_scr, kept_sem).start()
    for acc in (dbc, y, gb, fr):
        if acc is not None:
            acc[...] = jnp.zeros_like(acc)
    at = CHUNKS if mode == 2 else 2 * CHUNKS
    late = copies[at : at + CHUNKS]
    for cp in copies[:at] + copies[at + CHUNKS :]:
        cp.wait()

    def rows(s):
        return pl.ds(pl.multiple_of(s * 8, 8), 8)

    def wide(v):
        return jnp.concatenate([v] * KT, axis=1)

    def fold(v):
        return sum(v[:, 128 * i : 128 * i + 128] for i in range(KT))

    def loop(body, init):
        def outer(k, carry):
            for u in range(UNROLL):
                carry = body(k * UNROLL + u, carry)
            return carry

        return lax.fori_loop(0, S // UNROLL, outer, init)

    dsum = lax.fori_loop(0, S, lambda s, a: a + ddec[s], jnp.zeros((8, L), f32))

    def group(g, _):
        kk = lax.broadcasted_iota(jnp.int32, (2 * NN, NG * 128), 0)
        ln = lax.broadcasted_iota(jnp.int32, (2 * NN, NG * 128), 1) // 128
        Xb = jnp.where(kk == g * NG + ln, 1.0, 0.0).astype(bf16)
        Xc = jnp.where(kk == NN + g * NG + ln, 1.0, 0.0).astype(bf16)
        rr = lax.broadcasted_iota(jnp.int32, (NG * 128, 128), 0) // 128
        cc = lax.broadcasted_iota(jnp.int32, (NG * 128, 128), 1)
        Rb = jnp.where(cc == rr + g * NG, 1.0, 0.0).astype(bf16)
        Rc = jnp.where(cc == rr + NN + g * NG, 1.0, 0.0).astype(bf16)
        v = bc[...].reshape(S * CHUNKS, 128)[:, : 2 * NN]
        hi = v.astype(bf16)
        lo = (v - hi.astype(f32)).astype(bf16)
        bb[...] = dot(hi, Xb) + dot(lo, Xb)
        cb[...] = dot(hi, Xc) + dot(lo, Xc)

        def reduce(R):
            out = dot(q[...].astype(bf16), R)
            dbc[...] += out.reshape(S, CHUNKS, 128)

        r2 = [jnp.broadcast_to(rate2[pl.ds(g * NG + n, 1), :], (8, L)) for n in range(NG)]
        rt = [jnp.broadcast_to(rate[pl.ds(g * NG + n, 1), :], (8, L)) for n in range(NG)]
        total = [jnp.exp2(dsum * r2[n]) for n in range(NG)]
        zero = tuple(jnp.zeros((8, L), f32) for _ in range(NG))
        cols = [slice(128 * n, 128 * n + 128) for n in range(NG)]

        def ahead(s, st):
            d, x, b = ddec[s], dx[s], bb[rows(s), :]
            return tuple(
                jnp.exp2(d * r2[n]) * st[n] + x * wide(b[:, cols[n]]) for n in range(NG)
            )

        def forward(s, st):
            d, x, b, c, dst = ddec[s], dx[s], bb[rows(s), :], cb[rows(s), :], ds[s]
            acc, new = y[s], []
            for n in range(NG):
                p = jnp.exp2(d * r2[n]) * st[n]
                p_scr[s, n] = p
                h = p + x * wide(b[:, cols[n]])
                acc = acc + wide(c[:, cols[n]]) * h
                q[rows(s), cols[n]] = fold(dst * h)
                new.append(h)
            y[s] = acc
            return tuple(new)

        def behind(k, A):
            s = S - 1 - k
            d, c, dst = ddec[s], cb[rows(s), :], ds[s]
            return tuple(
                jnp.exp2(d * r2[n]) * (dst * wide(c[:, cols[n]]) + A[n]) for n in range(NG)
            )

        def backward(k, carry):
            A, dr = carry
            s = S - 1 - k
            d, x, b, c, dst = ddec[s], dx[s], bb[rows(s), :], cb[rows(s), :], ds[s]
            ga, fa, nA, ndr = gb[s], fr[s], [], []
            for n in range(NG):
                G = dst * wide(c[:, cols[n]]) + A[n]
                nA.append(jnp.exp2(d * r2[n]) * G)
                flow = G * p_scr[s, n]
                ndr.append(dr[n] + flow * d)
                fa = fa + flow * rt[n]
                ga = ga + G * wide(b[:, cols[n]])
                q[rows(s), cols[n]] = fold(G * x)
            gb[s] = ga
            fr[s] = fa
            return tuple(nA), tuple(ndr)

        if ahead_too:
            st = loop(ahead, zero)
            st = tuple(chain(st[n], total[n], False) for n in range(NG))
            if mode == 1:

                @pl.when(g > 0)
                def _():
                    pltpu.make_async_copy(p_scr, kept_h.at[g - 1], kept_sem).wait()

            @pl.when(g == 0)
            def _():
                for cp in late:
                    cp.wait()

            loop(forward, st)
            if mode == 1:
                pltpu.make_async_copy(p_scr, kept_h.at[g], kept_sem).start()
            reduce(Rc)
        if back_too:
            A = loop(behind, zero)
            A = tuple(chain(A[n], total[n], True) for n in range(NG))
            if mode == 2:
                pltpu.make_async_copy(kept_h.at[g], p_scr, kept_sem).wait()

                @pl.when(g == 0)
                def _():
                    for cp in late:
                        cp.wait()

            A, dr = loop(backward, (A, zero))
            if mode == 2:

                @pl.when(g + 1 < groups)
                def _():
                    pltpu.make_async_copy(kept_h.at[g + 1], p_scr, kept_sem).start()

            reduce(Rb)
            for n in range(NG):
                drate[pl.ds(g * NG + n, 1), :] = jnp.sum(dr[n], axis=0, keepdims=True)
        return 0

    lax.fori_loop(0, groups, group, 0)
    copies = []
    for a, (src, dst) in enumerate(((y, y_h), (gb, gb_h), (fr, fr_h), (dbc, dbc_h))):
        if src is None:
            continue
        for c in range(CHUNKS):
            copies.append(
                pltpu.make_async_copy(src.at[:, c, :], dst.at[pl.ds(c * S, S), :], sems.at[a, c])
            )
    for cp in copies:
        cp.start()
    if mode == 1:
        pltpu.make_async_copy(p_scr, kept_h.at[groups - 1], kept_sem).wait()
    for cp in copies:
        cp.wait()


def scan(mode, ddec, dx, ds, bc, rate, kept=None, NG=4):
    T, E = ddec.shape
    N = rate.shape[0]
    S = T // CHUNKS
    act = pltpu.VMEM((S, CHUNKS, E), f32)
    thin = pltpu.VMEM((S, CHUNKS, 128), f32)
    row, states = sds((T, E), f32), sds((N // NG, S, NG, CHUNKS, E), f32)
    outs, specs = [], []
    if mode != 2:
        outs, specs = outs + [row], specs + [HBM]
    if mode != 1:
        outs, specs = outs + [row, row, sds((N, E), f32)], specs + [HBM, HBM, VMEM]
    outs, specs = outs + [sds((T, 128), f32)], specs + [HBM]
    if mode == 1:
        outs, specs = outs + [states], specs + [HBM]
    return pl.pallas_call(
        functools.partial(scan_kernel, S, NG, mode),
        in_specs=[HBM] * 4 + [VMEM] * 2 + ([HBM] if mode == 2 else []),
        out_specs=specs,
        out_shape=outs,
        scratch_shapes=[act] * 3 + [thin] * 2
        + [pltpu.VMEM((S, NG, CHUNKS, E), f32)]
        + [pltpu.VMEM((T, NG * 128), f32)] * 3
        + [pltpu.SemaphoreType.DMA((4, CHUNKS)), pltpu.SemaphoreType.DMA]
        + [act] * ((mode != 2) + 2 * (mode != 1)),
        compiler_params=pltpu.CompilerParams(vmem_limit_bytes=60 << 20),
        cost_estimate=busy((114.0, 62.0, 68.0)[mode] * T * E * N / (2048 * 512 * 16), 24 * T * E),
        name=("scan_both", "scan_ahead", "scan_back")[mode],
    )(ddec, dx, ds, bc, rate * LOG2E, rate, *([kept] if mode == 2 else []))


def sum_kernel(pairs, n, *refs):
    parts, outs, rest = refs[:n], refs[n : 2 * n], refs[2 * n :]
    half, near, mine, far = rest[:n], rest[n : 2 * n], rest[2 * n : 3 * n], rest[3 * n : 4 * n]
    sems_s, sems_r = rest[4 * n :]
    T = parts[0].shape[1]
    H = T // 2
    Q = H // pairs
    me = lax.axis_index("chan")
    core, z = lax.rem(me, 2), me // 2
    mate = me + 1 - 2 * core
    peers = [lax.rem(z + k, pairs) for k in range(1, pairs)]
    gate = pltpu.get_barrier_semaphore()
    for dev in [mate] + [2 * p + core for p in peers]:
        pl.semaphore_signal(gate, inc=1, device_id={"chan": dev}, device_id_type=MESH)
    pl.semaphore_wait(gate, pairs)

    def cols(i, n):
        return pl.ds(pl.multiple_of(i * n, n), n)

    def send(a, src, dst, k, dev):
        c = pltpu.make_async_remote_copy(
            src_ref=src, dst_ref=dst, send_sem=sems_s.at[a, k], recv_sem=sems_r.at[a, k],
            device_id={"chan": dev}, device_id_type=MESH,
        )
        c.start()
        return c

    first = [send(a, parts[a].at[:, cols(1 - core, H)], near[a], 0, mate) for a in range(n)]
    for a in range(n):
        first[a].wait()
        half[a][...] = (
            parts[a][:, cols(core, H)].astype(f32) + near[a][...].astype(f32)
        ).astype(half[a].dtype)
    sends = [
        [send(a, half[a].at[:, cols(p, Q)], far[a].at[k], 1 + k, 2 * p + core) for a in range(n)]
        for k, p in enumerate(peers)
    ]
    totals = [half[a][:, cols(z, Q)].astype(f32) for a in range(n)]
    for k in range(pairs - 1):
        for a in range(n):
            sends[k][a].wait()
            totals[a] = totals[a] + far[a][k].astype(f32)
    at = pl.ds(pl.multiple_of(core * H + z * Q, Q), Q)
    sends = []
    for a in range(n):
        mine[a][...] = totals[a].astype(mine[a].dtype)
        for k, p in enumerate(peers):
            sends.append(send(a, mine[a], outs[a].at[:, at], pairs + k, 2 * p + core))
        outs[a][:, at] = mine[a][...]
    for c in sends:
        c.wait()
    last = [
        send(a, outs[a].at[:, cols(core, H)], outs[a].at[:, cols(core, H)], 2 * pairs - 1, mate)
        for a in range(n)
    ]
    for c in last:
        c.wait()


def chan_sum(parts, number):
    n = len(parts)
    T = parts[0].shape[1]
    pairs = lax.axis_size("chan") // 2
    Q = T // 2 // pairs
    if Q % 128:
        return [lax.psum(p.astype(f32), "chan").astype(p.dtype) for p in parts]
    shapes = [(p.shape[0], p.dtype) for p in parts]
    return pl.pallas_call(
        functools.partial(sum_kernel, pairs, n),
        in_specs=[VMEM] * n,
        out_specs=[VMEM] * n,
        out_shape=[sds(p.shape, p.dtype) for p in parts],
        scratch_shapes=[pltpu.VMEM((c, T // 2), d) for c, d in shapes] * 2
        + [pltpu.VMEM((c, Q), d) for c, d in shapes]
        + [pltpu.VMEM((pairs - 1, c, Q), d) for c, d in shapes]
        + [pltpu.SemaphoreType.DMA((n, 2 * pairs))] * 2,
        compiler_params=pltpu.CompilerParams(
            collective_id=number, has_side_effects=True, vmem_limit_bytes=32 << 20
        ),
        cost_estimate=busy(26.0, 4 * T),
        name="chan_sum",
    )(*parts)


def places(lens, block):
    t = lax.broadcasted_iota(jnp.int32, (RB, 1), 0) + block * RB
    begins = jnp.zeros_like(t)
    end = jnp.int32(0)
    start_of_padding = end
    for k in range(lens.shape[0]):
        start_of_padding = end
        end = end + lens[k]
        begins = begins + jnp.where(end <= t, lens[k], 0)
    return t - begins, jnp.where(t < start_of_padding, 1.0, 0.0)


def silu(v):
    return v * jax.nn.sigmoid(v)


def dot(a, b):
    return jnp.dot(a, b, preferred_element_type=f32)


def dot_nt(a, b):
    return lax.dot_general(a, b, (((1,), (1,)), ((), ())), preferred_element_type=f32)


def cut(ws, dim):
    at = 0
    for w in ws:
        yield slice(at, at + w.shape[dim]), w
        at += w.shape[dim]


def dot_tn(a, b):
    return lax.dot_general(a, b, (((0,), (0,)), ((), ())), preferred_element_type=f32)


def conv_of(xe, cw, cb, position, taps):
    conv = jnp.zeros((RB, cw.shape[1]), f32) + cb[...]
    lags = []
    for k in range(taps):
        lag = xe[pl.ds(8 - k, RB), :]
        lags.append(lag)
        conv = conv + cw[k : k + 1, :] * lag * jnp.where(position >= k, 1.0, 0.0)
    return conv, lags


def in_kernel(taps, kinds, lens, g, xw, cw, cb, *rest):
    ws, (x_o, gate_o, xc_o, low_o, thin_o, xe) = rest[:-6], rest[-6:]
    blk = pl.program_id(0)
    inner = cw.shape[1]
    mixed = sum(dot(g[:, at], w[0]) for at, w in cut(ws, 1))
    x = mixed[:, :inner]
    x_o[...] = x
    gate_o[...] = mixed[:, inner:]

    @pl.when(blk == 0)
    def _():
        xe[pl.ds(0, 8), :] = jnp.zeros((8, inner), f32)

    @pl.when(blk > 0)
    def _():
        xe[pl.ds(0, 8), :] = xe[pl.ds(RB, 8), :]

    xe[pl.ds(8, RB), :] = x
    position, valid = places(lens, blk)
    conv, lags = conv_of(xe, cw, cb, position, taps)
    xc = silu(conv).astype(bf16)
    xc_o[...] = xc
    part = dot_nt(xw[0], xc)
    rank = low_o.shape[0]
    low_o[...] = part[:rank].astype(bf16)
    thin_o[...] = part[rank:]


def mid_kernel(kinds, lens, u, gate, xc, low, thin, dtw, dtb, *rest):
    ws, (ddec_o, delta_o, dx_o, ds_o, dy_o, bc_o) = rest[:-6], rest[-6:]
    blk = pl.program_id(0)
    dy = sum(dot_nt(u[:, at], w[0]) for at, w in cut(ws, 2))
    position, valid = places(lens, blk)
    pre = dot_tn(low[...], dtw[0]) + dtb[...]
    delta = jnp.maximum(pre, 0.0) + jnp.log1p(jnp.exp(-jnp.abs(pre)))
    ddec_o[...] = jnp.where(position > 0, delta, RESET)
    delta_o[...] = delta
    dx_o[...] = delta * xc[...].astype(f32)
    ds_o[...] = dy * silu(gate[...]) * valid
    dy_o[...] = dy
    bc_o[...] = jnp.concatenate([thin[...], jnp.zeros((128 - thin.shape[0], RB), f32)], axis=0).T


def post_kernel(kinds, lens, y, dy, gate, xc, skip, *rest):
    ws, (out_o, y_o, dgate_o) = rest[:-3], rest[-3:]
    position, valid = places(lens, pl.program_id(0))
    z = gate[...]
    scanned = y[...] + skip[...] * xc[...].astype(f32)
    yo = (scanned * silu(z) * valid).astype(bf16)
    y_o[...] = yo
    dgate_o[...] = (dy[...] * scanned * valid * dsilu(z)).astype(bf16)
    for at, w in cut(ws, 2):
        out_o[:, at] = dot(yo, w[0]).astype(bf16)


def step_kernel(nbc, kinds, lens, gb, fr, ds, xc, delta, dbc, dbc2, skip, dtw, dpre_o, dxc_o, dpp_o, sum_o):
    x = xc[...].astype(f32)
    dl = delta[...]
    g = gb[...]
    dpre = ((x * g + fr[...]) * (1.0 - jnp.exp(-dl))).astype(bf16)
    dpre_o[...] = dpre
    dlow = dot_nt(dtw[0], dpre)
    both = (dbc[...] + dbc2[...]).T
    dpp_o[...] = jnp.concatenate([dlow, both[:nbc, :]], axis=0).astype(bf16)
    d = ds[...]
    dxc_o[...] = d * skip[...] + dl * g

    @pl.when(pl.program_id(0) == 0)
    def _():
        sum_o[...] = jnp.zeros_like(sum_o)

    sum_o[0:1, :] += jnp.sum(d * x, axis=0, keepdims=True)
    sum_o[1:2, :] += jnp.sum(dpre.astype(f32), axis=0, keepdims=True)


def back_kernel(taps, nblk, kinds, lens, dproj, xw, dxc, x, xprev, cw, cb, dgate, g, *rest):
    ws, (din_o, dn_o, sum_o, gain_o, xe, mk) = rest[:-6], rest[-6:]
    step = pl.program_id(0)
    blk = nblk - 1 - step
    inner = cw.shape[1]
    position, valid = places(lens, blk)
    xe[pl.ds(0, 8), :] = jnp.where(blk > 0, xprev[...], 0.0)
    xe[pl.ds(8, RB), :] = x[...]
    conv, lags = conv_of(xe, cw, cb, position, taps)
    dconv = (dxc[...] + dot_tn(dproj[...], xw[0])) * dsilu(conv)

    @pl.when(step == 0)
    def _():
        sum_o[...] = jnp.zeros_like(sum_o)
        gain_o[...] = jnp.zeros_like(gain_o)
        mk[:, pl.ds(RB, 8), :] = jnp.zeros((taps, 8, inner), f32)

    @pl.when(step > 0)
    def _():
        mk[:, pl.ds(RB, 8), :] = mk[:, pl.ds(0, 8), :]

    din = jnp.zeros((RB, inner), f32)
    for k in range(taps):
        masked = dconv * jnp.where(position >= k, 1.0, 0.0)
        mk[k, pl.ds(0, RB), :] = masked
        sum_o[k : k + 1, :] += jnp.sum(masked * lags[k], axis=0, keepdims=True)
        din = din + cw[k : k + 1, :] * mk[k, pl.ds(k, RB), :]
    sum_o[taps : taps + 1, :] += jnp.sum(dconv, axis=0, keepdims=True)
    din_o[...] = din.astype(bf16)
    dmix = jnp.concatenate([din.astype(bf16), dgate[...]], axis=1)
    for at, w in cut(ws, 1):
        part = dot_nt(dmix, w[0])
        dn_o[:, at] = part.astype(bf16)
        gain_o[0:1, at] += jnp.sum(part * g[:, at].astype(f32), axis=0, keepdims=True)


def stage(kernel, name, T, blocked, weights, whole, outs, sums, scratch, kinds, lens, us, reverse=False, prev=None, order=None, across={}, out_across=()):
    n = T // RB
    at = (lambda b: n - 1 - b) if reverse else (lambda b: b)
    per = MBLK // RB
    row = lambda b, kinds, lens: (at(b), 0)
    const = lambda b, kinds, lens: (0, 0)
    specs = {}
    args = {}
    col = lambda b, kinds, lens: (0, at(b))
    for key, a in blocked.items():
        specs[key], args[key] = pl.BlockSpec((RB, a.shape[1]), row), a
    for key, a in across.items():
        specs[key], args[key] = pl.BlockSpec((a.shape[0], RB), col), a
    for key, a in weights.items():
        specs[key] = pl.BlockSpec((1,) + a.shape[1:], lambda b, kinds, lens: (kinds[at(b) // per], 0, 0))
        args[key] = a
    for key, a in whole.items():
        specs[key], args[key] = pl.BlockSpec(a.shape, const), a
    if prev is not None:
        key, a = prev
        specs[key] = pl.BlockSpec((8, a.shape[1]), lambda b, kinds, lens: (jnp.maximum(at(b) * (RB // 8) - 1, 0), 0))
        args[key] = a
    out_specs = [pl.BlockSpec((RB, c), row) for c, _ in outs] + [pl.BlockSpec((c, RB), col) for c, _ in out_across] + [pl.BlockSpec(shape, const) for shape in sums]
    out_shape = [sds((T, c), dtype) for c, dtype in outs] + [sds((c, T), dtype) for c, dtype in out_across] + [sds(shape, f32) for shape in sums]
    nbytes = sum(a.size * a.dtype.itemsize for a in blocked.values()) + sum(T * c * 4 for c, _ in outs)
    return pl.pallas_call(
        kernel,
        grid_spec=pltpu.PrefetchScalarGridSpec(
            num_scalar_prefetch=2,
            grid=(n,),
            in_specs=[specs[k] for k in order],
            out_specs=out_specs,
            scratch_shapes=scratch,
        ),
        out_shape=out_shape,
        compiler_params=pltpu.CompilerParams(vmem_limit_bytes=56 << 20),
        cost_estimate=busy(us, nbytes),
        name=name,
    )(kinds, lens, *[args[k] for k in order])


def swap(v, bits, axis="seq"):
    n = lax.axis_size(axis)
    return lax.ppermute(v, axis, [(i, i ^ bits) for i in range(n)])


def gather_all(own):
    return [own] + [swap(own, j) for j in range(1, lax.axis_size("seq"))]


def gather_near(own):
    return [own] + [swap(own, j) for j in range(1, 3)] if lax.axis_size("seq") == 4 else gather_all(own)


def gather_far(blocks, dim):
    if lax.axis_size("seq") != 4:
        return blocks
    own, by_x, by_y = blocks
    first, second = jnp.split(by_x, 2, axis=dim)[0], jnp.split(by_y, 2, axis=dim)[1]
    return [own, by_x, by_y, swap(first, 2), swap(second, 1)]


def scatter_far(parts):
    if len(parts) != 4:
        return []
    half = parts[3].shape[1] // 2
    return [swap(parts[3][:, :half], 1), swap(parts[3][:, half:], 2)]


def scatter_near(parts, far):
    if len(parts) != 4:
        return scatter_all(parts)
    own, for_x, for_y, _ = parts
    a, b = far
    half = a.shape[1]
    for_y = jnp.concatenate(
        [(for_y[:, :half].astype(f32) + a.astype(f32)).astype(bf16), for_y[:, half:]], axis=1
    )
    for_x = jnp.concatenate(
        [for_x[:, :half], (for_x[:, half:].astype(f32) + b.astype(f32)).astype(bf16)], axis=1
    )
    return [own, swap(for_x, 1), swap(for_y, 2)]


def scatter_all(parts):
    return [parts[0]] + [swap(p, j) for j, p in enumerate(parts) if j]


def total_of(terms):
    return sum(t.astype(f32) for t in terms)


def seq_sum(v):
    return v + sum(swap(v, j) for j in range(1, lax.axis_size("seq")))


def chan_gather(v):
    me = lax.axis_index("chan")
    bit = 1
    while bit < lax.axis_size("chan"):
        other = swap(v, bit, "chan")
        up = (me & bit) > 0
        v = jnp.concatenate([jnp.where(up, other, v), jnp.where(up, v, other)], axis=1)
        bit *= 2
    return v


def chan_scatter(v):
    me = lax.axis_index("chan")
    bit = lax.axis_size("chan") // 2
    while bit:
        low, high = jnp.split(v, 2, axis=1)
        up = (me & bit) > 0
        v = jnp.where(up, high, low) + swap(jnp.where(up, low, high), bit, "chan")
        bit //= 2
    return v


def square_order(v, me):
    n = lax.axis_size("seq")
    parts = jnp.split(v, n, axis=-1)
    bit = 1
    while bit < n:
        on = (me & bit) > 0
        parts = [jnp.where(on, parts[i ^ bit], parts[i]) for i in range(n)]
        bit *= 2
    return jnp.concatenate(parts, axis=-1)


def shards(
    hidden, out_grad, modality, lengths, in_weight, x_weight, dt_weight, out_weight,
    conv_weight, conv_bias, a_log, d_skip, dt_bias, norm_gain
):
    micro, rows, width = hidden.shape
    T = modality.shape[1]
    inner = conv_bias.shape[0]
    nstate = a_log.shape[0]
    taps = conv_weight.shape[0]
    me = lax.axis_index("seq")
    nseq = lax.axis_size("seq")
    kinds_all = modality[:, ::MBLK]
    flat = kinds_all.reshape(-1)
    rate = -jnp.exp(a_log)
    P4 = in_weight.shape[1]
    w_own, norm_gain = lax.optimization_barrier(
        (in_weight.reshape(MODES, P4, 2 * inner), norm_gain)
    )
    w_in = gather_near(w_own)
    gain = chan_gather(norm_gain[None, :])[0]
    x_small = jnp.swapaxes(x_weight, 1, 2)
    ncols = x_small.shape[1]
    scales, units, normed, flipped = [], [], [], []
    for i in range(micro):
        source = hidden[i].astype(f32)
        scale = lax.rsqrt(jnp.mean(source * source, axis=1, keepdims=True) + 1e-05)
        unit = source * scale
        normed.append(square_order((unit * gain[None, :]).astype(bf16), me))
        flipped.append(square_order(out_grad[i], me))
        scales.append(scale)
        units.append(unit)
    small = jnp.concatenate([x_small, dt_weight], axis=1)
    small = jnp.concatenate([small] + [swap(small, b) for b in range(1, nseq)], axis=2)
    small = square_order(small, me)
    x_full = jnp.concatenate(jnp.split(small[:, :ncols], nseq, axis=2), axis=1)
    dt_full = jnp.concatenate(jnp.split(small[:, ncols:], nseq, axis=2), axis=1)
    rank = dt_full.shape[1]
    w_in[1], w_in[2], x_full, dt_full = lax.optimization_barrier((w_in[1], w_in[2], x_full, dt_full))
    w_in = gather_far(w_in, 1)
    later, w_in[-1] = lax.optimization_barrier((out_weight, w_in[-1]))
    w_out = gather_near(later)
    gathered = [lax.all_gather(normed[0], "chan", axis=0, tiled=True)]
    ups = [lax.all_gather(flipped[0], "chan", axis=0, tiled=True)]
    win = {f"w{j}": w for j, w in enumerate(w_in)}
    ws = list(win)
    vec = dict(cw=conv_weight, cb=conv_bias[None, :])
    skip, dtb = d_skip[None, :], dt_bias[None, :]
    branches, dn_parts, sums = [], [], []
    t_out, t_gate, t_x, t_dt, t_xw, d_ins = [], [], [], [], [], []

    def finish(c, d_proj):
        i = c["i"]
        d_in, dn_part, sum_b, sum_g = stage(
            functools.partial(back_kernel, taps, T // RB), "back_stage", T,
            dict(dxc=c["dxc"], x=c["x"], dgate=c["dgate"], g=gathered[i]), dict(**win, xw=x_full), vec,
            [(inner, bf16), (width, bf16)], [(8, inner), (8, width)],
            [pltpu.VMEM((RB + 8, inner), f32), pltpu.VMEM((taps, RB + 8, inner), f32)],
            kinds_all[i], lengths[i, 0], 26.0,
            reverse=True, prev=("xprev", c["x"]),
            order=["dproj", "xw", "dxc", "x", "xprev", "cw", "cb", "dgate", "g", *ws],
            across=dict(dproj=d_proj),
        )
        d_ins.append(d_in)
        t_xw.extend(by_tile([d_proj], [c["xc"]], 1, f32))
        sums.append((c["sum_a"], sum_b, c["s_rate"] * rate, sum_g[:1]))
        return dn_part

    carried = None
    for i in range(micro):
        kinds, lens = kinds_all[i], lengths[i, 0]
        if carried is not None:
            gathered[i], d_part = lax.optimization_barrier((gathered[i], d_part))
        x_in, gate, xc, low_part, bc_part = stage(
            functools.partial(in_kernel, taps), "in_stage", T,
            dict(g=gathered[i]), dict(**win, xw=x_full), vec,
            [(inner, f32), (inner, f32), (inner, bf16)], [],
            [pltpu.VMEM((RB + 8, inner), f32)], kinds, lens, 21.0,
            order=["g", "xw", "cw", "cb", *ws],
            out_across=((rank, bf16), (2 * nstate, f32)),
        )
        if carried is None:
            low, thin = chan_sum([low_part, bc_part], 0)
            low, normed, flipped, w_out = lax.optimization_barrier((low, normed, flipped, w_out))
            wout = {f"w{j}": w for j, w in enumerate(gather_far(w_out, 2))}
            wo = list(wout)
            for j in range(1, micro):
                gathered.append(lax.all_gather(normed[j], "chan", axis=0, tiled=True))
                ups.append(lax.all_gather(flipped[j], "chan", axis=0, tiled=True))
        else:
            low, thin, d_proj = chan_sum([low_part, bc_part, d_part], 1)
            low, out_part = lax.optimization_barrier((low, out_part))
            branches.append(lax.psum_scatter(out_part, "chan", scatter_dimension=0, tiled=True))
            dn_part = finish(carried, d_proj)
            thin, dn_part = lax.optimization_barrier((thin, dn_part))
            dn_parts.append(lax.psum_scatter(dn_part, "chan", scatter_dimension=0, tiled=True))
        ddec, delta, dx, ds, dy, bc = stage(
            mid_kernel, "mid_stage", T,
            dict(u=ups[i], gate=gate, xc=xc), dict(**wout, dtw=dt_full), dict(dtb=dtb),
            [(inner, f32)] * 5 + [(128, f32)], [], [], kinds, lens, 19.0,
            order=["u", "gate", "xc", "low", "thin", "dtw", "dtb", *wo], across=dict(low=low, thin=thin),
        )
        whole = i < micro - 1
        if whole:
            y, gb, fr, s_rate, dbc = scan(0, ddec, dx, ds, bc, rate)
            dbc2 = jnp.zeros_like(dbc)
        else:
            y, dbc, kept = scan(1, ddec, dx, ds, bc, rate)
        if dn_parts:
            y, branches = lax.optimization_barrier((y, branches))
        out_part, y_out, d_gate = stage(
            post_kernel, "post_stage", T,
            dict(y=y, dy=dy, gate=gate, xc=xc), dict(**wout), dict(skip=skip),
            [(width, bf16), (inner, bf16), (inner, bf16)], [], [], kinds, lens, 14.0,
            order=["y", "dy", "gate", "xc", "skip", *wo],
        )
        if not whole:
            branches.append(lax.psum_scatter(out_part, "chan", scatter_dimension=0, tiled=True))
        t_out += by_tile([y_out], [ups[i]], 0)
        t_gate += by_tile([gathered[i]], [d_gate], 0)
        if not whole:
            g_out = by_modality_blocks(flat, t_out, 1, nseq)
            g_gate = by_modality_blocks(flat, t_gate, 0, nseq)
            far = scatter_far(g_out)
            t_x = by_tile(gathered[:-1], d_ins, 0)
            bc, far, g_gate[-1], dn_parts, t_x = lax.optimization_barrier(
                (bc, far, g_gate[-1], dn_parts, t_x)
            )
            g_out = scatter_near(g_out, far)
            gb, fr, s_rate, dbc2 = scan(2, ddec, dx, ds, bc, rate, kept)
            far = scatter_far(g_gate)
            dbc2, far, g_out = lax.optimization_barrier((dbc2, far, g_out))
            g_gate = scatter_near(g_gate, far)
        d_pre, dxc, d_part, sum_a = stage(
            functools.partial(step_kernel, 2 * nstate), "step_stage", T,
            dict(gb=gb, fr=fr, ds=ds, xc=xc, delta=delta, dbc=dbc, dbc2=dbc2), dict(dtw=dt_full), dict(skip=skip),
            [(inner, bf16), (inner, f32)], [(8, inner)], [], kinds, lens, 12.0,
            order=["gb", "fr", "ds", "xc", "delta", "dbc", "dbc2", "skip", "dtw"],
            out_across=((x_full.shape[1], bf16),),
        )
        t_dt += by_tile([low], [d_pre], 1, f32)
        carried = dict(i=i, dxc=dxc, x=x_in, dgate=d_gate, xc=xc, sum_a=sum_a, s_rate=s_rate)
    (d_proj,) = chan_sum([d_part], 2)
    d_proj, g_gate = lax.optimization_barrier((d_proj, g_gate))
    dn_part = finish(carried, d_proj)
    dn_part, branches[-1] = lax.optimization_barrier((dn_part, branches[-1]))
    dn_parts.append(lax.psum_scatter(dn_part, "chan", scatter_dimension=0, tiled=True))
    t_x += by_tile(gathered[-1:], d_ins[-1:], 0)
    g_x = by_modality_blocks(flat, t_x, 0, nseq)
    far = scatter_far(g_x)
    totals = [sum(s[j] for s in sums) for j in range(4)]
    far, t_dt, t_xw, g_out, g_gate, totals = lax.optimization_barrier(
        (far, t_dt, t_xw, g_out, g_gate, totals)
    )
    g_x = scatter_near(g_x, far)
    gain_rows = square_order(totals[3], me).reshape(-1, inner)
    vectors = seq_sum(jnp.concatenate([*totals[:3], gain_rows], axis=0))
    gain_total = chan_scatter(vectors[-gain_rows.shape[0] :].reshape(1, width))[0] / norm_gain
    g_dt = by_modality(flat, t_dt)
    g_xw = by_modality(flat, t_xw)
    ndt = dt_weight.shape[1]

    def seat_rows(bits):
        seat = me ^ bits
        a = lax.dynamic_slice_in_dim(g_xw, seat * ncols, ncols, 1)
        b = lax.dynamic_slice_in_dim(g_dt, seat * ndt, ndt, 1)
        return jnp.concatenate([a, b], axis=1)

    g_small = scatter_all([seat_rows(b) for b in range(nseq)])
    outputs, input_grads = [], []
    for i in range(micro):
        branch = square_order(branches[i].astype(f32), me)
        outputs.append((hidden[i].astype(f32) + branch).astype(bf16))
        d_unit = square_order(dn_parts[i].astype(f32), me) * gain[None, :]
        input_grads.append(
            scales[i] * (d_unit - units[i] * jnp.mean(d_unit * units[i], axis=1, keepdims=True))
            + out_grad[i].astype(f32)
        )
    outputs, input_grads = jnp.stack(outputs, axis=0), jnp.stack(input_grads, axis=0)
    g_out, g_gate, g_small = total_of(g_out), total_of(g_gate), total_of(g_small)
    g_x, outputs, input_grads, g_out, g_gate = lax.optimization_barrier(
        (g_x, outputs, input_grads, g_out, g_gate)
    )
    g_x = total_of(g_x)
    is_x = lax.broadcasted_iota(jnp.int32, (1, 1, 2, 1), 2) == 0
    g_in = jnp.where(is_x, g_x[:, :, None, :], g_gate[:, :, None, :])
    return (
        outputs,
        input_grads,
        g_in,
        jnp.swapaxes(g_small[:, :ncols], 1, 2),
        g_small[:, ncols:],
        g_out,
        vectors[8 : 8 + taps],
        vectors[8 + taps],
        vectors[16 : 16 + nstate],
        vectors[0],
        vectors[1],
        gain_total,
    )


def solution(mesh):
    act = P(None, ("seq", "chan"), None)
    weights = (P(None, "seq", None, "chan"), P(None, "chan", "seq"), P(None, "seq", "chan"), P(None, "chan", "seq"))
    vectors = (P(None, "chan"), P("chan"), P(None, "chan"), P("chan"), P("chan"), P("chan"))
    return jax.shard_map(
        shards,
        mesh=mesh,
        in_specs=(act, act, P(None, "seq"), P(None, "seq", None), *weights, *vectors),
        out_specs=(act, act, *weights, *vectors),
        check_vma=False,
    )
```

```python
import functools

import jax
import jax.numpy as jnp
from jax import lax
from jax.experimental import pallas as pl
from jax.experimental.pallas import tpu as pltpu
from jax.sharding import PartitionSpec as P

MODES = 3
MBLK = 1024
LOG2E = 1.4426950408889634
RESET = 1.0e4
CHUNKS = 8
UNROLL = 8
EARLY = 0.2
RB = 512

f32, bf16 = jnp.float32, jnp.bfloat16
HBM = pl.BlockSpec(memory_space=pl.ANY)
VMEM = pl.BlockSpec(memory_space=pltpu.VMEM)
MESH = pl.DeviceIdType.MESH


def sds(shape, dtype):
    return jax.ShapeDtypeStruct(shape, dtype)


def cost(flops, nbytes, trans=0):
    return pl.CostEstimate(flops=int(flops), bytes_accessed=int(nbytes), transcendentals=int(trans))


def busy(us, nbytes):
    return cost(us * EARLY * 1.1e9, nbytes * EARLY)


def dsilu(value):
    sig = jax.nn.sigmoid(value)
    return sig * (1.0 + value * (1.0 - sig))


def by_tile(lefts, rights, left_dim, dtype=bf16):
    out = []
    for left, right in zip(lefts, rights):
        for t in range(right.shape[0] // MBLK):
            a = lax.slice_in_dim(left, t * MBLK, t * MBLK + MBLK, axis=left_dim)
            b = lax.slice_in_dim(right, t * MBLK, t * MBLK + MBLK, axis=0)
            dims = (((left_dim,), (0,)), ((), ()))
            out.append(lax.dot_general(a, b, dims, preferred_element_type=f32).astype(dtype))
    return out


def by_modality(kinds, tiles):
    out = []
    for m in range(MODES):
        out.append(
            sum(jnp.where(kinds[t] == m, tile.astype(f32), 0.0) for t, tile in enumerate(tiles)).astype(bf16)
        )
    return jnp.stack(out)


def by_modality_blocks(kinds, tiles, dim, n):
    blocks = [jnp.split(tile, n, axis=dim) for tile in tiles]
    return [by_modality(kinds, [b[j] for b in blocks]) for j in range(n)]


def chain(ends, total, back):
    row = lax.broadcasted_iota(jnp.int32, ends.shape, 0)
    for k in (1, 2, 4):
        shift = CHUNKS - k if back else k
        ok = (row < CHUNKS - k) if back else (row >= k)
        ends = ends + total * jnp.where(ok, pltpu.roll(ends, shift, 0), 0.0)
        total = total * jnp.where(ok, pltpu.roll(total, shift, 0), 1.0)
    shift = CHUNKS - 1 if back else 1
    ok = (row < CHUNKS - 1) if back else (row >= 1)
    return jnp.where(ok, pltpu.roll(ends, shift, 0), 0.0)


def scan_kernel(S, NG, mode, *refs):
    ahead_too, back_too = mode != 2, mode != 1
    ins, refs = refs[:4], refs[4:]
    rate2, rate, refs = refs[0], refs[1], refs[2:]
    kept_h = None
    if mode == 2:
        kept_h, refs = refs[0], refs[1:]
    y_h = gb_h = fr_h = drate = y = gb = fr = None
    if ahead_too:
        y_h, refs = refs[0], refs[1:]
    if back_too:
        gb_h, fr_h, drate, refs = refs[0], refs[1], refs[2], refs[3:]
    dbc_h, refs = refs[0], refs[1:]
    if mode == 1:
        kept_h, refs = refs[0], refs[1:]
    ddec, dx, ds, bc, dbc, p_scr, bb, cb, q, sems, kept_sem = refs[:11]
    refs = refs[11:]
    if ahead_too:
        y, refs = refs[0], refs[1:]
    if back_too:
        gb, fr = refs
    NN, L = rate.shape
    KT = L // 128
    groups = NN // NG
    copies = []
    for a, (src, dst) in enumerate(zip(ins, (ddec, dx, ds, bc))):
        for c in range(CHUNKS):
            copies.append(
                pltpu.make_async_copy(src.at[pl.ds(c * S, S), :], dst.at[:, c, :], sems.at[a, c])
            )
    for cp in copies:
        cp.start()
    if mode == 2:
        pltpu.make_async_copy(kept_h.at[0], p_scr, kept_sem).start()
    for acc in (dbc, y, gb, fr):
        if acc is not None:
            acc[...] = jnp.zeros_like(acc)
    at = CHUNKS if mode == 2 else 2 * CHUNKS
    late = copies[at : at + CHUNKS]
    for cp in copies[:at] + copies[at + CHUNKS :]:
        cp.wait()

    def rows(s):
        return pl.ds(pl.multiple_of(s * 8, 8), 8)

    def wide(v):
        return jnp.concatenate([v] * KT, axis=1)

    def fold(v):
        return sum(v[:, 128 * i : 128 * i + 128] for i in range(KT))

    def loop(body, init):
        def outer(k, carry):
            for u in range(UNROLL):
                carry = body(k * UNROLL + u, carry)
            return carry

        return lax.fori_loop(0, S // UNROLL, outer, init)

    dsum = lax.fori_loop(0, S, lambda s, a: a + ddec[s], jnp.zeros((8, L), f32))

    def group(g, _):
        kk = lax.broadcasted_iota(jnp.int32, (2 * NN, NG * 128), 0)
        ln = lax.broadcasted_iota(jnp.int32, (2 * NN, NG * 128), 1) // 128
        Xb = jnp.where(kk == g * NG + ln, 1.0, 0.0).astype(bf16)
        Xc = jnp.where(kk == NN + g * NG + ln, 1.0, 0.0).astype(bf16)
        rr = lax.broadcasted_iota(jnp.int32, (NG * 128, 128), 0) // 128
        cc = lax.broadcasted_iota(jnp.int32, (NG * 128, 128), 1)
        Rb = jnp.where(cc == rr + g * NG, 1.0, 0.0).astype(bf16)
        Rc = jnp.where(cc == rr + NN + g * NG, 1.0, 0.0).astype(bf16)
        v = bc[...].reshape(S * CHUNKS, 128)[:, : 2 * NN]
        hi = v.astype(bf16)
        lo = (v - hi.astype(f32)).astype(bf16)
        bb[...] = dot(hi, Xb) + dot(lo, Xb)
        cb[...] = dot(hi, Xc) + dot(lo, Xc)

        def reduce(R):
            out = dot(q[...].astype(bf16), R)
            dbc[...] += out.reshape(S, CHUNKS, 128)

        r2 = [jnp.broadcast_to(rate2[pl.ds(g * NG + n, 1), :], (8, L)) for n in range(NG)]
        rt = [jnp.broadcast_to(rate[pl.ds(g * NG + n, 1), :], (8, L)) for n in range(NG)]
        total = [jnp.exp2(dsum * r2[n]) for n in range(NG)]
        zero = tuple(jnp.zeros((8, L), f32) for _ in range(NG))
        cols = [slice(128 * n, 128 * n + 128) for n in range(NG)]

        def ahead(s, st):
            d, x, b = ddec[s], dx[s], bb[rows(s), :]
            return tuple(
                jnp.exp2(d * r2[n]) * st[n] + x * wide(b[:, cols[n]]) for n in range(NG)
            )

        def forward(s, st):
            d, x, b, c, dst = ddec[s], dx[s], bb[rows(s), :], cb[rows(s), :], ds[s]
            acc, new = y[s], []
            for n in range(NG):
                p = jnp.exp2(d * r2[n]) * st[n]
                p_scr[s, n] = p
                h = p + x * wide(b[:, cols[n]])
                acc = acc + wide(c[:, cols[n]]) * h
                q[rows(s), cols[n]] = fold(dst * h)
                new.append(h)
            y[s] = acc
            return tuple(new)

        def behind(k, A):
            s = S - 1 - k
            d, c, dst = ddec[s], cb[rows(s), :], ds[s]
            return tuple(
                jnp.exp2(d * r2[n]) * (dst * wide(c[:, cols[n]]) + A[n]) for n in range(NG)
            )

        def backward(k, carry):
            A, dr = carry
            s = S - 1 - k
            d, x, b, c, dst = ddec[s], dx[s], bb[rows(s), :], cb[rows(s), :], ds[s]
            ga, fa, nA, ndr = gb[s], fr[s], [], []
            for n in range(NG):
                G = dst * wide(c[:, cols[n]]) + A[n]
                nA.append(jnp.exp2(d * r2[n]) * G)
                flow = G * p_scr[s, n]
                ndr.append(dr[n] + flow * d)
                fa = fa + flow * rt[n]
                ga = ga + G * wide(b[:, cols[n]])
                q[rows(s), cols[n]] = fold(G * x)
            gb[s] = ga
            fr[s] = fa
            return tuple(nA), tuple(ndr)

        if ahead_too:
            st = loop(ahead, zero)
            st = tuple(chain(st[n], total[n], False) for n in range(NG))
            if mode == 1:

                @pl.when(g > 0)
                def _():
                    pltpu.make_async_copy(p_scr, kept_h.at[g - 1], kept_sem).wait()

            @pl.when(g == 0)
            def _():
                for cp in late:
                    cp.wait()

            loop(forward, st)
            if mode == 1:
                pltpu.make_async_copy(p_scr, kept_h.at[g], kept_sem).start()
            reduce(Rc)
        if back_too:
            A = loop(behind, zero)
            A = tuple(chain(A[n], total[n], True) for n in range(NG))
            if mode == 2:
                pltpu.make_async_copy(kept_h.at[g], p_scr, kept_sem).wait()

                @pl.when(g == 0)
                def _():
                    for cp in late:
                        cp.wait()

            A, dr = loop(backward, (A, zero))
            if mode == 2:

                @pl.when(g + 1 < groups)
                def _():
                    pltpu.make_async_copy(kept_h.at[g + 1], p_scr, kept_sem).start()

            reduce(Rb)
            for n in range(NG):
                drate[pl.ds(g * NG + n, 1), :] = jnp.sum(dr[n], axis=0, keepdims=True)
        return 0

    lax.fori_loop(0, groups, group, 0)
    copies = []
    for a, (src, dst) in enumerate(((y, y_h), (gb, gb_h), (fr, fr_h), (dbc, dbc_h))):
        if src is None:
            continue
        for c in range(CHUNKS):
            copies.append(
                pltpu.make_async_copy(src.at[:, c, :], dst.at[pl.ds(c * S, S), :], sems.at[a, c])
            )
    for cp in copies:
        cp.start()
    if mode == 1:
        pltpu.make_async_copy(p_scr, kept_h.at[groups - 1], kept_sem).wait()
    for cp in copies:
        cp.wait()


def scan(mode, ddec, dx, ds, bc, rate, kept=None, NG=4):
    T, E = ddec.shape
    N = rate.shape[0]
    S = T // CHUNKS
    act = pltpu.VMEM((S, CHUNKS, E), f32)
    thin = pltpu.VMEM((S, CHUNKS, 128), f32)
    row, states = sds((T, E), f32), sds((N // NG, S, NG, CHUNKS, E), f32)
    outs, specs = [], []
    if mode != 2:
        outs, specs = outs + [row], specs + [HBM]
    if mode != 1:
        outs, specs = outs + [row, row, sds((N, E), f32)], specs + [HBM, HBM, VMEM]
    outs, specs = outs + [sds((T, 128), f32)], specs + [HBM]
    if mode == 1:
        outs, specs = outs + [states], specs + [HBM]
    return pl.pallas_call(
        functools.partial(scan_kernel, S, NG, mode),
        in_specs=[HBM] * 4 + [VMEM] * 2 + ([HBM] if mode == 2 else []),
        out_specs=specs,
        out_shape=outs,
        scratch_shapes=[act] * 3 + [thin] * 2
        + [pltpu.VMEM((S, NG, CHUNKS, E), f32)]
        + [pltpu.VMEM((T, NG * 128), f32)] * 3
        + [pltpu.SemaphoreType.DMA((4, CHUNKS)), pltpu.SemaphoreType.DMA]
        + [act] * ((mode != 2) + 2 * (mode != 1)),
        compiler_params=pltpu.CompilerParams(vmem_limit_bytes=60 << 20),
        cost_estimate=busy((114.0, 62.0, 68.0)[mode] * T * E * N / (2048 * 512 * 16), 24 * T * E),
        name=("scan_both", "scan_ahead", "scan_back")[mode],
    )(ddec, dx, ds, bc, rate * LOG2E, rate, *([kept] if mode == 2 else []))


def sum_kernel(pairs, n, *refs):
    parts, outs, rest = refs[:n], refs[n : 2 * n], refs[2 * n :]
    half, near, mine, far = rest[:n], rest[n : 2 * n], rest[2 * n : 3 * n], rest[3 * n : 4 * n]
    sems_s, sems_r = rest[4 * n :]
    T = parts[0].shape[1]
    H = T // 2
    Q = H // pairs
    me = lax.axis_index("chan")
    core, z = lax.rem(me, 2), me // 2
    mate = me + 1 - 2 * core
    peers = [lax.rem(z + k, pairs) for k in range(1, pairs)]
    gate = pltpu.get_barrier_semaphore()
    for dev in [mate] + [2 * p + core for p in peers]:
        pl.semaphore_signal(gate, inc=1, device_id={"chan": dev}, device_id_type=MESH)
    pl.semaphore_wait(gate, pairs)

    def cols(i, n):
        return pl.ds(pl.multiple_of(i * n, n), n)

    def send(a, src, dst, k, dev):
        c = pltpu.make_async_remote_copy(
            src_ref=src, dst_ref=dst, send_sem=sems_s.at[a, k], recv_sem=sems_r.at[a, k],
            device_id={"chan": dev}, device_id_type=MESH,
        )
        c.start()
        return c

    first = [send(a, parts[a].at[:, cols(1 - core, H)], near[a], 0, mate) for a in range(n)]
    sends = []
    for a in range(n):
        first[a].wait()
        half[a][...] = (
            parts[a][:, cols(core, H)].astype(f32) + near[a][...].astype(f32)
        ).astype(half[a].dtype)
        sends.append(
            [send(a, half[a].at[:, cols(p, Q)], far[a].at[k], 1 + k, 2 * p + core) for k, p in enumerate(peers)]
        )
    at = pl.ds(pl.multiple_of(core * H + z * Q, Q), Q)
    back = []
    for a in range(n):
        total = half[a][:, cols(z, Q)].astype(f32)
        for k in range(pairs - 1):
            sends[a][k].wait()
            total = total + far[a][k].astype(f32)
        mine[a][...] = total.astype(mine[a].dtype)
        back.append(
            [send(a, mine[a], outs[a].at[:, at], pairs + k, 2 * p + core) for k, p in enumerate(peers)]
        )
        outs[a][:, at] = mine[a][...]
    last = []
    for a in range(n):
        for c in back[a]:
            c.wait()
        done = outs[a].at[:, cols(core, H)]
        last.append(send(a, done, done, 2 * pairs - 1, mate))
    for c in last:
        c.wait()


def chan_sum(parts, number):
    n = len(parts)
    T = parts[0].shape[1]
    pairs = lax.axis_size("chan") // 2
    Q = T // 2 // pairs
    if Q % 128:
        return [lax.psum(p.astype(f32), "chan").astype(p.dtype) for p in parts]
    shapes = [(p.shape[0], p.dtype) for p in parts]
    return pl.pallas_call(
        functools.partial(sum_kernel, pairs, n),
        in_specs=[VMEM] * n,
        out_specs=[VMEM] * n,
        out_shape=[sds(p.shape, p.dtype) for p in parts],
        scratch_shapes=[pltpu.VMEM((c, T // 2), d) for c, d in shapes] * 2
        + [pltpu.VMEM((c, Q), d) for c, d in shapes]
        + [pltpu.VMEM((pairs - 1, c, Q), d) for c, d in shapes]
        + [pltpu.SemaphoreType.DMA((n, 2 * pairs))] * 2,
        compiler_params=pltpu.CompilerParams(
            collective_id=number, has_side_effects=True, vmem_limit_bytes=32 << 20
        ),
        cost_estimate=busy(26.0, 4 * T),
        name="chan_sum",
    )(*parts)


def places(lens, block):
    t = lax.broadcasted_iota(jnp.int32, (RB, 1), 0) + block * RB
    begins = jnp.zeros_like(t)
    end = jnp.int32(0)
    start_of_padding = end
    for k in range(lens.shape[0]):
        start_of_padding = end
        end = end + lens[k]
        begins = begins + jnp.where(end <= t, lens[k], 0)
    return t - begins, jnp.where(t < start_of_padding, 1.0, 0.0)


def silu(v):
    return v * jax.nn.sigmoid(v)


def dot(a, b):
    return jnp.dot(a, b, preferred_element_type=f32)


def dot_nt(a, b):
    return lax.dot_general(a, b, (((1,), (1,)), ((), ())), preferred_element_type=f32)


def cut(ws, dim):
    at = 0
    for w in ws:
        yield slice(at, at + w.shape[dim]), w
        at += w.shape[dim]


def dot_tn(a, b):
    return lax.dot_general(a, b, (((0,), (0,)), ((), ())), preferred_element_type=f32)


def conv_of(xe, cw, cb, position, taps):
    conv = jnp.zeros((RB, cw.shape[1]), f32) + cb[...]
    lags = []
    for k in range(taps):
        lag = xe[pl.ds(8 - k, RB), :]
        lags.append(lag)
        conv = conv + cw[k : k + 1, :] * lag * jnp.where(position >= k, 1.0, 0.0)
    return conv, lags


def in_kernel(taps, kinds, lens, g, xw, cw, cb, *rest):
    ws, (x_o, gate_o, xc_o, low_o, thin_o, xe) = rest[:-6], rest[-6:]
    blk = pl.program_id(0)
    inner = cw.shape[1]
    mixed = sum(dot(g[:, at], w[0]) for at, w in cut(ws, 1))
    x = mixed[:, :inner]
    x_o[...] = x
    gate_o[...] = mixed[:, inner:]

    @pl.when(blk == 0)
    def _():
        xe[pl.ds(0, 8), :] = jnp.zeros((8, inner), f32)

    @pl.when(blk > 0)
    def _():
        xe[pl.ds(0, 8), :] = xe[pl.ds(RB, 8), :]

    xe[pl.ds(8, RB), :] = x
    position, valid = places(lens, blk)
    conv, lags = conv_of(xe, cw, cb, position, taps)
    xc = silu(conv).astype(bf16)
    xc_o[...] = xc
    part = dot_nt(xw[0], xc)
    rank = low_o.shape[0]
    low_o[...] = part[:rank].astype(bf16)
    thin_o[...] = part[rank:]


def mid_kernel(kinds, lens, u, gate, xc, low, thin, dtw, dtb, *rest):
    ws, (ddec_o, delta_o, dx_o, ds_o, dy_o, bc_o) = rest[:-6], rest[-6:]
    blk = pl.program_id(0)
    dy = sum(dot_nt(u[:, at], w[0]) for at, w in cut(ws, 2))
    position, valid = places(lens, blk)
    pre = dot_tn(low[...], dtw[0]) + dtb[...]
    delta = jnp.maximum(pre, 0.0) + jnp.log1p(jnp.exp(-jnp.abs(pre)))
    ddec_o[...] = jnp.where(position > 0, delta, RESET)
    delta_o[...] = delta
    dx_o[...] = delta * xc[...].astype(f32)
    ds_o[...] = dy * silu(gate[...]) * valid
    dy_o[...] = dy
    bc_o[...] = jnp.concatenate([thin[...], jnp.zeros((128 - thin.shape[0], RB), f32)], axis=0).T


def post_kernel(kinds, lens, y, dy, gate, xc, skip, *rest):
    ws, (out_o, y_o, dgate_o) = rest[:-3], rest[-3:]
    position, valid = places(lens, pl.program_id(0))
    z = gate[...]
    scanned = y[...] + skip[...] * xc[...].astype(f32)
    yo = (scanned * silu(z) * valid).astype(bf16)
    y_o[...] = yo
    dgate_o[...] = (dy[...] * scanned * valid * dsilu(z)).astype(bf16)
    for at, w in cut(ws, 2):
        out_o[:, at] = dot(yo, w[0]).astype(bf16)


def step_kernel(nbc, kinds, lens, gb, fr, ds, xc, delta, dbc, dbc2, skip, dtw, dpre_o, dxc_o, dpp_o, sum_o):
    x = xc[...].astype(f32)
    dl = delta[...]
    g = gb[...]
    dpre = ((x * g + fr[...]) * (1.0 - jnp.exp(-dl))).astype(bf16)
    dpre_o[...] = dpre
    dlow = dot_nt(dtw[0], dpre)
    both = (dbc[...] + dbc2[...]).T
    dpp_o[...] = jnp.concatenate([dlow, both[:nbc, :]], axis=0).astype(bf16)
    d = ds[...]
    dxc_o[...] = d * skip[...] + dl * g

    @pl.when(pl.program_id(0) == 0)
    def _():
        sum_o[...] = jnp.zeros_like(sum_o)

    sum_o[0:1, :] += jnp.sum(d * x, axis=0, keepdims=True)
    sum_o[1:2, :] += jnp.sum(dpre.astype(f32), axis=0, keepdims=True)


def back_kernel(taps, nblk, kinds, lens, dproj, xw, dxc, x, xprev, cw, cb, dgate, g, *rest):
    ws, (din_o, dn_o, sum_o, gain_o, xe, mk) = rest[:-6], rest[-6:]
    step = pl.program_id(0)
    blk = nblk - 1 - step
    inner = cw.shape[1]
    position, valid = places(lens, blk)
    xe[pl.ds(0, 8), :] = jnp.where(blk > 0, xprev[...], 0.0)
    xe[pl.ds(8, RB), :] = x[...]
    conv, lags = conv_of(xe, cw, cb, position, taps)
    dconv = (dxc[...] + dot_tn(dproj[...], xw[0])) * dsilu(conv)

    @pl.when(step == 0)
    def _():
        sum_o[...] = jnp.zeros_like(sum_o)
        gain_o[...] = jnp.zeros_like(gain_o)
        mk[:, pl.ds(RB, 8), :] = jnp.zeros((taps, 8, inner), f32)

    @pl.when(step > 0)
    def _():
        mk[:, pl.ds(RB, 8), :] = mk[:, pl.ds(0, 8), :]

    din = jnp.zeros((RB, inner), f32)
    for k in range(taps):
        masked = dconv * jnp.where(position >= k, 1.0, 0.0)
        mk[k, pl.ds(0, RB), :] = masked
        sum_o[k : k + 1, :] += jnp.sum(masked * lags[k], axis=0, keepdims=True)
        din = din + cw[k : k + 1, :] * mk[k, pl.ds(k, RB), :]
    sum_o[taps : taps + 1, :] += jnp.sum(dconv, axis=0, keepdims=True)
    din_o[...] = din.astype(bf16)
    dmix = jnp.concatenate([din.astype(bf16), dgate[...]], axis=1)
    for at, w in cut(ws, 1):
        part = dot_nt(dmix, w[0])
        dn_o[:, at] = part.astype(bf16)
        gain_o[0:1, at] += jnp.sum(part * g[:, at].astype(f32), axis=0, keepdims=True)


def stage(kernel, name, T, blocked, weights, whole, outs, sums, scratch, kinds, lens, us, reverse=False, prev=None, order=None, across={}, out_across=()):
    n = T // RB
    at = (lambda b: n - 1 - b) if reverse else (lambda b: b)
    per = MBLK // RB
    row = lambda b, kinds, lens: (at(b), 0)
    const = lambda b, kinds, lens: (0, 0)
    specs = {}
    args = {}
    col = lambda b, kinds, lens: (0, at(b))
    for key, a in blocked.items():
        specs[key], args[key] = pl.BlockSpec((RB, a.shape[1]), row), a
    for key, a in across.items():
        specs[key], args[key] = pl.BlockSpec((a.shape[0], RB), col), a
    for key, a in weights.items():
        specs[key] = pl.BlockSpec((1,) + a.shape[1:], lambda b, kinds, lens: (kinds[at(b) // per], 0, 0))
        args[key] = a
    for key, a in whole.items():
        specs[key], args[key] = pl.BlockSpec(a.shape, const), a
    if prev is not None:
        key, a = prev
        specs[key] = pl.BlockSpec((8, a.shape[1]), lambda b, kinds, lens: (jnp.maximum(at(b) * (RB // 8) - 1, 0), 0))
        args[key] = a
    out_specs = [pl.BlockSpec((RB, c), row) for c, _ in outs] + [pl.BlockSpec((c, RB), col) for c, _ in out_across] + [pl.BlockSpec(shape, const) for shape in sums]
    out_shape = [sds((T, c), dtype) for c, dtype in outs] + [sds((c, T), dtype) for c, dtype in out_across] + [sds(shape, f32) for shape in sums]
    nbytes = sum(a.size * a.dtype.itemsize for a in blocked.values()) + sum(T * c * 4 for c, _ in outs)
    return pl.pallas_call(
        kernel,
        grid_spec=pltpu.PrefetchScalarGridSpec(
            num_scalar_prefetch=2,
            grid=(n,),
            in_specs=[specs[k] for k in order],
            out_specs=out_specs,
            scratch_shapes=scratch,
        ),
        out_shape=out_shape,
        compiler_params=pltpu.CompilerParams(vmem_limit_bytes=56 << 20),
        cost_estimate=busy(us, nbytes),
        name=name,
    )(kinds, lens, *[args[k] for k in order])


def swap(v, bits, axis="seq"):
    n = lax.axis_size(axis)
    return lax.ppermute(v, axis, [(i, i ^ bits) for i in range(n)])


def gather_all(own):
    return [own] + [swap(own, j) for j in range(1, lax.axis_size("seq"))]


def gather_near(own):
    return [own] + [swap(own, j) for j in range(1, 3)] if lax.axis_size("seq") == 4 else gather_all(own)


def gather_far(blocks, dim):
    if lax.axis_size("seq") != 4:
        return blocks
    own, by_x, by_y = blocks
    first, second = jnp.split(by_x, 2, axis=dim)[0], jnp.split(by_y, 2, axis=dim)[1]
    return [own, by_x, by_y, swap(first, 2), swap(second, 1)]


def scatter_all(parts):
    return [parts[0]] + [swap(p, j) for j, p in enumerate(parts) if j]


def scatter_far(parts):
    if len(parts) != 4:
        return []
    half = parts[3].shape[1] // 2
    return [swap(parts[3][:, :half], 1), swap(parts[3][:, half:], 2)]


def with_far(parts, far):
    if len(parts) != 4:
        return parts
    own, for_x, for_y, _ = parts
    a, b = far
    half = a.shape[1]
    for_y = jnp.concatenate(
        [(for_y[:, :half].astype(f32) + a.astype(f32)).astype(bf16), for_y[:, half:]], axis=1
    )
    for_x = jnp.concatenate(
        [for_x[:, :half], (for_x[:, half:].astype(f32) + b.astype(f32)).astype(bf16)], axis=1
    )
    return [own, for_x, for_y]


def scatter_near(parts, far):
    return scatter_all(with_far(parts, far))


def total_of(terms):
    return sum(t.astype(f32) for t in terms)


def seq_sum(v):
    return v + sum(swap(v, j) for j in range(1, lax.axis_size("seq")))


def chan_gather(v):
    me = lax.axis_index("chan")
    bit = 1
    while bit < lax.axis_size("chan"):
        other = swap(v, bit, "chan")
        up = (me & bit) > 0
        v = jnp.concatenate([jnp.where(up, other, v), jnp.where(up, v, other)], axis=1)
        bit *= 2
    return v


def chan_scatter(v):
    me = lax.axis_index("chan")
    bit = lax.axis_size("chan") // 2
    while bit:
        low, high = jnp.split(v, 2, axis=1)
        up = (me & bit) > 0
        v = jnp.where(up, high, low) + swap(jnp.where(up, low, high), bit, "chan")
        bit //= 2
    return v


def square_order(v, me):
    n = lax.axis_size("seq")
    parts = jnp.split(v, n, axis=-1)
    bit = 1
    while bit < n:
        on = (me & bit) > 0
        parts = [jnp.where(on, parts[i ^ bit], parts[i]) for i in range(n)]
        bit *= 2
    return jnp.concatenate(parts, axis=-1)


def shards(
    hidden, out_grad, modality, lengths, in_weight, x_weight, dt_weight, out_weight,
    conv_weight, conv_bias, a_log, d_skip, dt_bias, norm_gain
):
    micro, rows, width = hidden.shape
    T = modality.shape[1]
    inner = conv_bias.shape[0]
    nstate = a_log.shape[0]
    taps = conv_weight.shape[0]
    me = lax.axis_index("seq")
    nseq = lax.axis_size("seq")
    kinds_all = modality[:, ::MBLK]
    flat = kinds_all.reshape(-1)
    rate = -jnp.exp(a_log)
    P4 = in_weight.shape[1]
    w_own, norm_gain = lax.optimization_barrier(
        (in_weight.reshape(MODES, P4, 2 * inner), norm_gain)
    )
    w_in = gather_near(w_own)
    gain = chan_gather(norm_gain[None, :])[0]
    x_small = jnp.swapaxes(x_weight, 1, 2)
    ncols = x_small.shape[1]
    scales, units, normed, flipped = [], [], [], []
    for i in range(micro):
        source = hidden[i].astype(f32)
        scale = lax.rsqrt(jnp.mean(source * source, axis=1, keepdims=True) + 1e-05)
        unit = source * scale
        normed.append(square_order((unit * gain[None, :]).astype(bf16), me))
        flipped.append(square_order(out_grad[i], me))
        scales.append(scale)
        units.append(unit)
    small = jnp.concatenate([x_small, dt_weight], axis=1)
    small = jnp.concatenate([small] + [swap(small, b) for b in range(1, nseq)], axis=2)
    small = square_order(small, me)
    x_full = jnp.concatenate(jnp.split(small[:, :ncols], nseq, axis=2), axis=1)
    dt_full = jnp.concatenate(jnp.split(small[:, ncols:], nseq, axis=2), axis=1)
    rank = dt_full.shape[1]
    w_in[1], w_in[2], x_full, dt_full = lax.optimization_barrier((w_in[1], w_in[2], x_full, dt_full))
    w_in = gather_far(w_in, 1)
    later, w_in[-1] = lax.optimization_barrier((out_weight, w_in[-1]))
    w_out = gather_near(later)
    gathered = [lax.all_gather(normed[0], "chan", axis=0, tiled=True)]
    ups = [lax.all_gather(flipped[0], "chan", axis=0, tiled=True)]
    win = {f"w{j}": w for j, w in enumerate(w_in)}
    ws = list(win)
    vec = dict(cw=conv_weight, cb=conv_bias[None, :])
    skip, dtb = d_skip[None, :], dt_bias[None, :]
    branches, dn_parts, sums = [], [], []
    t_out, t_gate, t_x, t_dt, t_xw, d_ins = [], [], [], [], [], []

    def finish(c, d_proj):
        i = c["i"]
        d_in, dn_part, sum_b, sum_g = stage(
            functools.partial(back_kernel, taps, T // RB), "back_stage", T,
            dict(dxc=c["dxc"], x=c["x"], dgate=c["dgate"], g=gathered[i]), dict(**win, xw=x_full), vec,
            [(inner, bf16), (width, bf16)], [(8, inner), (8, width)],
            [pltpu.VMEM((RB + 8, inner), f32), pltpu.VMEM((taps, RB + 8, inner), f32)],
            kinds_all[i], lengths[i, 0], 26.0,
            reverse=True, prev=("xprev", c["x"]),
            order=["dproj", "xw", "dxc", "x", "xprev", "cw", "cb", "dgate", "g", *ws],
            across=dict(dproj=d_proj),
        )
        d_ins.append(d_in)
        t_xw.extend(by_tile([d_proj], [c["xc"]], 1, f32))
        sums.append((c["sum_a"], sum_b, c["s_rate"] * rate, sum_g[:1]))
        return dn_part

    carried = None
    for i in range(micro):
        kinds, lens = kinds_all[i], lengths[i, 0]
        if carried is not None:
            gathered[i], d_part = lax.optimization_barrier((gathered[i], d_part))
        x_in, gate, xc, low_part, bc_part = stage(
            functools.partial(in_kernel, taps), "in_stage", T,
            dict(g=gathered[i]), dict(**win, xw=x_full), vec,
            [(inner, f32), (inner, f32), (inner, bf16)], [],
            [pltpu.VMEM((RB + 8, inner), f32)], kinds, lens, 21.0,
            order=["g", "xw", "cw", "cb", *ws],
            out_across=((rank, bf16), (2 * nstate, f32)),
        )
        if carried is None:
            low, thin = chan_sum([low_part, bc_part], 0)
            low, normed, flipped, w_out = lax.optimization_barrier((low, normed, flipped, w_out))
            wout = {f"w{j}": w for j, w in enumerate(gather_far(w_out, 2))}
            wo = list(wout)
            for j in range(1, micro):
                gathered.append(lax.all_gather(normed[j], "chan", axis=0, tiled=True))
                ups.append(lax.all_gather(flipped[j], "chan", axis=0, tiled=True))
        else:
            low, thin, d_proj = chan_sum([low_part, bc_part, d_part], 1)
            low, out_part = lax.optimization_barrier((low, out_part))
            branches.append(lax.psum_scatter(out_part, "chan", scatter_dimension=0, tiled=True))
            dn_part = finish(carried, d_proj)
            thin, dn_part = lax.optimization_barrier((thin, dn_part))
            dn_parts.append(lax.psum_scatter(dn_part, "chan", scatter_dimension=0, tiled=True))
        ddec, delta, dx, ds, dy, bc = stage(
            mid_kernel, "mid_stage", T,
            dict(u=ups[i], gate=gate, xc=xc), dict(**wout, dtw=dt_full), dict(dtb=dtb),
            [(inner, f32)] * 5 + [(128, f32)], [], [], kinds, lens, 19.0,
            order=["u", "gate", "xc", "low", "thin", "dtw", "dtb", *wo], across=dict(low=low, thin=thin),
        )
        whole = i < micro - 1
        if whole:
            y, gb, fr, s_rate, dbc = scan(0, ddec, dx, ds, bc, rate)
            dbc2 = jnp.zeros_like(dbc)
        else:
            y, dbc, kept = scan(1, ddec, dx, ds, bc, rate)
        if dn_parts:
            y, branches = lax.optimization_barrier((y, branches))
        out_part, y_out, d_gate = stage(
            post_kernel, "post_stage", T,
            dict(y=y, dy=dy, gate=gate, xc=xc), dict(**wout), dict(skip=skip),
            [(width, bf16), (inner, bf16), (inner, bf16)], [], [], kinds, lens, 14.0,
            order=["y", "dy", "gate", "xc", "skip", *wo],
        )
        if not whole:
            branches.append(lax.psum_scatter(out_part, "chan", scatter_dimension=0, tiled=True))
        t_out += by_tile([y_out], [ups[i]], 0)
        t_gate += by_tile([gathered[i]], [d_gate], 0)
        if not whole:
            g_out = by_modality_blocks(flat, t_out, 1, nseq)
            g_gate = by_modality_blocks(flat, t_gate, 0, nseq)
            far = scatter_far(g_out)
            t_x = by_tile(gathered[:-1], d_ins, 0)
            bc, far, g_gate[-1], dn_parts, t_x = lax.optimization_barrier(
                (bc, far, g_gate[-1], dn_parts, t_x)
            )
            g_out = scatter_near(g_out, far)
            gb, fr, s_rate, dbc2 = scan(2, ddec, dx, ds, bc, rate, kept)
            far = scatter_far(g_gate)
            dbc2, far, g_out = lax.optimization_barrier((dbc2, far, g_out))
            g_gate = scatter_near(g_gate, far)
        d_pre, dxc, d_part, sum_a = stage(
            functools.partial(step_kernel, 2 * nstate), "step_stage", T,
            dict(gb=gb, fr=fr, ds=ds, xc=xc, delta=delta, dbc=dbc, dbc2=dbc2), dict(dtw=dt_full), dict(skip=skip),
            [(inner, bf16), (inner, f32)], [(8, inner)], [], kinds, lens, 12.0,
            order=["gb", "fr", "ds", "xc", "delta", "dbc", "dbc2", "skip", "dtw"],
            out_across=((x_full.shape[1], bf16),),
        )
        t_dt += by_tile([low], [d_pre], 1, f32)
        carried = dict(i=i, dxc=dxc, x=x_in, dgate=d_gate, xc=xc, sum_a=sum_a, s_rate=s_rate)
    (d_proj,) = chan_sum([d_part], 2)
    d_proj, g_gate = lax.optimization_barrier((d_proj, g_gate))
    dn_part = finish(carried, d_proj)
    dn_part, branches[-1] = lax.optimization_barrier((dn_part, branches[-1]))
    dn_parts.append(lax.psum_scatter(dn_part, "chan", scatter_dimension=0, tiled=True))
    totals = [sum(s[j] for s in sums) for j in range(4)]
    gain_rows = square_order(totals[3], me).reshape(-1, inner)
    vectors = seq_sum(jnp.concatenate([*totals[:3], gain_rows], axis=0))
    gain_total = chan_scatter(vectors[-gain_rows.shape[0] :].reshape(1, width))[0] / norm_gain
    t_x += by_tile(gathered[-1:], d_ins[-1:], 0)
    g_x = by_modality_blocks(flat, t_x, 0, nseq)
    g_x[-1], vectors, gain_total = lax.optimization_barrier((g_x[-1], vectors, gain_total))
    far = scatter_far(g_x)
    g_x = with_far(g_x, far)
    g_x, t_dt, t_xw, g_out, g_gate = lax.optimization_barrier((g_x, t_dt, t_xw, g_out, g_gate))
    g_x = scatter_all(g_x)
    g_dt = by_modality(flat, t_dt)
    g_xw = by_modality(flat, t_xw)
    ndt = dt_weight.shape[1]

    def seat_rows(bits):
        seat = me ^ bits
        a = lax.dynamic_slice_in_dim(g_xw, seat * ncols, ncols, 1)
        b = lax.dynamic_slice_in_dim(g_dt, seat * ndt, ndt, 1)
        return jnp.concatenate([a, b], axis=1)

    g_small = scatter_all([seat_rows(b) for b in range(nseq)])
    outputs, input_grads = [], []
    for i in range(micro):
        branch = square_order(branches[i].astype(f32), me)
        outputs.append((hidden[i].astype(f32) + branch).astype(bf16))
        d_unit = square_order(dn_parts[i].astype(f32), me) * gain[None, :]
        input_grads.append(
            scales[i] * (d_unit - units[i] * jnp.mean(d_unit * units[i], axis=1, keepdims=True))
            + out_grad[i].astype(f32)
        )
    outputs, input_grads = jnp.stack(outputs, axis=0), jnp.stack(input_grads, axis=0)
    g_out, g_gate, g_small = total_of(g_out), total_of(g_gate), total_of(g_small)
    g_x, outputs, input_grads, g_out, g_gate = lax.optimization_barrier(
        (g_x, outputs, input_grads, g_out, g_gate)
    )
    g_x = total_of(g_x)
    is_x = lax.broadcasted_iota(jnp.int32, (1, 1, 2, 1), 2) == 0
    g_in = jnp.where(is_x, g_x[:, :, None, :], g_gate[:, :, None, :])
    return (
        outputs,
        input_grads,
        g_in,
        jnp.swapaxes(g_small[:, :ncols], 1, 2),
        g_small[:, ncols:],
        g_out,
        vectors[8 : 8 + taps],
        vectors[8 + taps],
        vectors[16 : 16 + nstate],
        vectors[0],
        vectors[1],
        gain_total,
    )


def solution(mesh):
    act = P(None, ("seq", "chan"), None)
    weights = (P(None, "seq", None, "chan"), P(None, "chan", "seq"), P(None, "seq", "chan"), P(None, "chan", "seq"))
    vectors = (P(None, "chan"), P("chan"), P(None, "chan"), P("chan"), P("chan"), P("chan"))
    return jax.shard_map(
        shards,
        mesh=mesh,
        in_specs=(act, act, P(None, "seq"), P(None, "seq", None), *weights, *vectors),
        out_specs=(act, act, *weights, *vectors),
        check_vma=False,
    )
```
